256 devices in a mesh: batch: 32 (over z_lo, x, core), patch: 8 (over z_hi, y).
Axes of the slice: x: 4, y: 4, z: 8 (z_hi: 2, z_lo: 4; z = z_hi * 4 + z_lo), core: 2. Of those that a mesh axis runs over, the one named last changes fastest.
Arguments:
- timestep: int32 [32], P('batch'), parts along dimension 0, may hold values from 0 to 999
- features: bfloat16 [98304, 640], P(('batch', 'patch')), parts along dimension 0, may hold values from -128 to 128
- hidden: bfloat16 [98304, 640], P(('batch', 'patch')), parts along dimension 0, may hold values from -20 to 20
- stale_hidden: bfloat16 [98304, 640], P(('batch', 'patch')), parts along dimension 0, may hold values from -6 to 6
- gn_gain: float32 [640], replicated, may hold values from 0.1 to 1.9
- gn_shift: float32 [640], replicated, may hold values from -3 to 3
- conv_kernel: bfloat16 [3, 3, 640, 640], replicated, may hold values from -0.078125 to 0.078125
- time_weight: bfloat16 [320, 640], replicated, may hold values from -0.3125 to 0.3125
- wq: bfloat16 [640, 640], replicated, may hold values from -0.355756237 to 0.355756237
- wk: bfloat16 [640, 640], replicated, may hold values from -0.237170825 to 0.237170825
- wv: bfloat16 [640, 640], replicated, may hold values from -0.25 to 0.25
Outputs:
- res_out: bfloat16 [98304, 640], P(('batch', 'patch')), parts along dimension 0
- attn_out: bfloat16 [98304, 640], P(('batch', 'patch')), parts along dimension 0
The draws below stay inside these ranges and needn't reach their ends.
There are 32 independent parts, one for each index of `batch`. The reference program is written for one: setup_inputs(seed, part) draws one part's arguments, and reference() takes and returns one part's arrays. A program takes and returns all parts, laid end to end along the dimension named above; an argument that names none is the same for every part. Nothing has to cross between parts.
All inputs are finite; a program needn't handle non-finite values.
Results may differ from the reference program's by a relative error of at most 0.0072.
Values may be sent and summed in bfloat16 or wider, within the bound.
A program may use at most 128 MiB of HBM per device.

```python
import math
import jax
import jax.numpy as jnp
from jax import lax

HEADS = 10
HEAD_DIM = 64
GROUPS = 16
TEMB = 320
W = 128
CH = 640
TOK_DEV = 384
TOKENS = 3072
H = 24
N_PATCH = 8


def shared_projection(key):
    return jnp.clip(jax.random.normal(key, (CH, CH), jnp.float32), -6.0, 6.0)


def draw_features(key, part):
    key = jax.random.fold_in(key, 11)
    key_noise, key_rows, key_cols, key_mean = jax.random.split(key, 4)
    position = jnp.arange(TOKENS, dtype=jnp.float32) / (TOKENS - 1)
    noise = jnp.clip(jax.random.normal(key_noise, (TOKENS, CH), jnp.float32), -5.0, 5.0)
    rising = jnp.exp(math.log(3.0) * position) / 1.7320508
    offset = 0.5
    row_scale = rising * jnp.exp(jax.random.uniform(key_rows, (TOKENS,), jnp.float32, -1.15, 1.15))
    col_scale = jnp.exp(jax.random.uniform(key_cols, (CH,), jnp.float32, -1.15, 1.15))
    common = offset * jax.random.uniform(key_mean, (CH,), jnp.float32, 0.5, 1.5)
    return ((noise + common[None, :]) * row_scale[:, None] * col_scale[None, :]).astype(jnp.bfloat16)


def draw_hidden(key, part):
    key = jax.random.fold_in(key, 23)
    key_noise = jax.random.fold_in(key, 0)
    result = jnp.clip(jax.random.normal(key_noise, (TOKENS, CH), jnp.float32), -5.0, 5.0)
    return result.astype(jnp.bfloat16)


def draw_wk(key, part):
    common = shared_projection(key)
    return (common * CH ** (-0.5)).astype(jnp.bfloat16)


def draw_wq(key, part):
    common = shared_projection(key)
    key = jax.random.fold_in(key, 37)
    own_part = jnp.clip(jax.random.normal(key, (CH, CH), jnp.float32), -6.0, 6.0)
    return ((0.6 * common + 0.8 * own_part) * CH ** (-0.5)).astype(jnp.bfloat16)


def shard_levels(stream_key, dims, pieces, smallest, largest):
    level, own = 1.0, jax.random.fold_in(stream_key, 6)
    for dim, blocks in pieces:
        steps = jnp.exp(jax.random.uniform(jax.random.fold_in(own, dim), (blocks,), jnp.float32, smallest / len(pieces), largest / len(pieces)))
        level = level * jnp.repeat(steps, dims[dim] // blocks).reshape([-1 if axis == dim else 1 for axis in range(len(dims))])
    return level


def bell_draw(stream_key, shape, width, bound, pieces=(), kind=jnp.bfloat16):
    entries = width * jax.random.normal(stream_key, shape, jnp.float32)
    if pieces:
        entries = entries * shard_levels(stream_key, shape, pieces, -0.22, 0.18)
    return jnp.clip(entries, -bound, bound).astype(kind)


def setup_inputs(seed: int = 0, part: int = 0) -> dict:
    keys = jax.random.split(jax.random.key(seed), 12)
    own_keys = jax.random.split(jax.random.fold_in(keys[11], part), 12)
    timestep = jax.random.randint(own_keys[0], (1,), 0, 1000).astype(jnp.int32)
    features = draw_features(jax.random.fold_in(jax.random.fold_in(keys[11], part), 71), part)
    hidden = draw_hidden(jax.random.fold_in(jax.random.fold_in(keys[11], part), 71), part)
    stale_hidden = bell_draw(own_keys[3], (TOKENS, CH), 1.0, 6.0, ((0, 8),))
    gn_gain = jnp.clip(1.0 + 0.18 * jax.random.normal(keys[4], (CH,), jnp.float32), 0.1, 1.9)
    gn_shift = bell_draw(keys[5], (CH,), 0.5, 3.0, (), jnp.float32)
    conv_kernel = bell_draw(keys[6], (3, 3, CH, CH), (9 * CH) ** -0.5, 0.078125)
    time_weight = bell_draw(keys[7], (TEMB, CH), TEMB ** -0.5, 0.3125)
    wq = draw_wq(jax.random.fold_in(keys[11], 71), part)
    wk = draw_wk(jax.random.fold_in(keys[11], 71), part)
    wv = bell_draw(keys[10], (CH, CH), CH ** -0.5, 0.25)
    return {"timestep": timestep, "features": features, "hidden": hidden, "stale_hidden": stale_hidden, "gn_gain": gn_gain, "gn_shift": gn_shift, "conv_kernel": conv_kernel, "time_weight": time_weight, "wq": wq, "wk": wk, "wv": wv}


epsilon = 1e-05

def group_norm_silu(features, gn_gain, gn_shift):
    values = features.astype(jnp.float32).reshape(TOKENS, GROUPS, CH // GROUPS)
    entry_count = TOKENS * (CH // GROUPS)
    group_mean = lax.optimization_barrier(jnp.sum(values, axis=(0, 2))) / entry_count
    centered = values - group_mean[None, :, None]
    variance = lax.optimization_barrier(jnp.sum(centered * centered, axis=(0, 2))) / entry_count
    normed = (centered * lax.rsqrt(variance + epsilon)[None, :, None]).reshape(TOKENS, CH)
    normed = normed * gn_gain[None, :] + gn_shift[None, :]
    return jax.nn.silu(normed).astype(jnp.bfloat16)

def convolve(activated, conv_kernel):
    latent_grid = activated.reshape(H, W, CH)
    padded = jnp.pad(latent_grid, ((1, 1), (1, 1), (0, 0)))
    running_sum = jnp.zeros((TOKENS, CH), jnp.float32)
    for row_offset in range(3):
        for col_offset in range(3):
            window = padded[row_offset:row_offset + H, col_offset:col_offset + W].reshape(TOKENS, CH)
            running_sum = running_sum + jnp.dot(window, conv_kernel[row_offset, col_offset], preferred_element_type=jnp.float32)
    return running_sum

def time_features(timestep):
    half_size = TEMB // 2
    frequencies = jnp.exp(-math.log(10000.0) * jnp.arange(half_size, dtype=jnp.float32) / half_size)
    angles = timestep.astype(jnp.float32)[0] * frequencies
    return jax.nn.silu(jnp.concatenate([jnp.cos(angles), jnp.sin(angles)])).astype(jnp.bfloat16)

def project(source, weight):
    return jnp.dot(source, weight, preferred_element_type=jnp.float32).astype(jnp.bfloat16)

def attention(hidden, stale_hidden, wq, wk, wv):
    queries = project(hidden, wq).reshape(N_PATCH, TOK_DEV, HEADS, HEAD_DIM)
    fresh_keys = project(hidden, wk)
    fresh_values = project(hidden, wv)
    stale_keys = project(stale_hidden, wk)
    stale_values = project(stale_hidden, wv)
    owner_patch = jnp.arange(TOKENS, dtype=jnp.int32) // TOK_DEV
    score_scale = 1.0 / math.sqrt(HEAD_DIM)

    def one_patch(inputs):
        patch_index, query_rows = inputs
        own_mask = (owner_patch == patch_index)[:, None]
        key_rows = jnp.where(own_mask, fresh_keys, stale_keys).reshape(TOKENS, HEADS, HEAD_DIM).astype(jnp.float32)
        value_rows = jnp.where(own_mask, fresh_values, stale_values).reshape(TOKENS, HEADS, HEAD_DIM).astype(jnp.float32)
        scores = jnp.einsum('qhd,khd->hqk', query_rows.astype(jnp.float32), key_rows) * score_scale
        row_max = lax.optimization_barrier(jnp.max(scores, axis=2, keepdims=True))
        weights = jnp.exp(scores - row_max)
        weight_sum = lax.optimization_barrier(jnp.sum(weights, axis=2))
        soft_weights = lax.optimization_barrier(weights.astype(jnp.bfloat16)).astype(jnp.float32)
        summed = jnp.einsum('hqk,khd->qhd', soft_weights, value_rows)
        return (summed / jnp.transpose(weight_sum)[:, :, None]).reshape(TOK_DEV, CH)
    output = lax.map(one_patch, (jnp.arange(N_PATCH, dtype=jnp.int32), queries))
    return output.reshape(TOKENS, CH).astype(jnp.bfloat16)

def reference(timestep, features, hidden, stale_hidden, gn_gain, gn_shift, conv_kernel, time_weight, wq, wk, wv):
    activated = group_norm_silu(features, gn_gain, gn_shift)
    time_embed = time_features(timestep)
    time_shift = jnp.dot(time_embed[None, :], time_weight, preferred_element_type=jnp.float32)
    res_out = (convolve(activated, conv_kernel) + time_shift).astype(jnp.bfloat16)
    attn_out = attention(hidden, stale_hidden, wq, wk, wv)
    return (res_out, attn_out)
```

```python
import functools
import math

import jax
import jax.numpy as jnp
from jax import lax
from jax.experimental import pallas as pl
from jax.experimental.pallas import tpu as pltpu
from jax.sharding import PartitionSpec as P

F32, BF16 = jnp.float32, jnp.bfloat16
MESH = pl.DeviceIdType.MESH
NT = (((1,), (1,)), ((), ()))
HIGHEST = lax.Precision.HIGHEST
TOK, CH, ROW, HALF = 384, 640, 128, 192
GROUPS, GROUP_CH, PATCHES, RING = 16, 40, 8, 4
PAIRS, PAIR_CH, PAIR_Q = 5, 128, 768
VROWS = 144
EPSILON = 1e-05
S_STAT_R, S_STAT_L, S_STAT_O, S_STAT_P, S_HALO_R, S_HALO_L, S_CORNER = range(7)
S_BULK = 7
N_SENDS = S_BULK + 14
R_STAT_L, R_STAT_R, R_STAT_O, R_STAT_P, R_TOP, R_BOTTOM, R_CORNER = range(7)
D_FEAT, D_HID, D_WQ, D_WK, D_WV, D_TW, D_CONV = range(7)


def kernel(
    timestep, feat_hbm, hid_hbm, stale_hbm, gain, shift, conv_hbm, tw_hbm, wq_hbm, wk_hbm, wv_hbm,
    res_ref, attn_ref,
    keys, feats, corner, stats, wq, wk, wv, wvt, tw, convw, act, qt, kbuf, vt, scores, probs,
    row_max, acc, conv_acc, send_sem, recv_sem, bulk_sem, load_sem,
):
    me = lax.axis_index("patch")
    y, zh = lax.rem(me, RING), lax.div(me, RING)
    right = {"patch": zh * RING + lax.rem(y + 1, RING)}
    left = {"patch": zh * RING + lax.rem(y + RING - 1, RING)}
    partner = {"patch": (1 - zh) * RING + y}

    barrier = pltpu.get_barrier_semaphore()
    for device in (right, left, partner):
        pl.semaphore_signal(barrier, inc=1, device_id=device, device_id_type=MESH)

    loads = [
        (D_FEAT, feat_hbm, feats.at[pl.ds(ROW, TOK)]),
        (D_HID, hid_hbm, keys.at[0]),
        (D_WQ, wq_hbm, wq),
        (D_WK, wk_hbm, wk),
        (D_WV, wv_hbm, wv),
        (D_TW, tw_hbm, tw),
        (D_CONV, conv_hbm, convw),
    ]
    load = {i: pltpu.make_async_copy(src, dst, load_sem.at[i]) for i, src, dst in loads}
    for i, _, _ in loads:
        load[i].start()

    def half(ref, h):
        return ref.at[pl.ds(h * HALF, HALF)]

    def remote(slot, src, dst, recv, device):
        return pltpu.make_async_remote_copy(
            src_ref=src, dst_ref=dst, send_sem=send_sem.at[slot], recv_sem=recv,
            device_id=device, device_id_type=MESH,
        )

    def key_half(step, h):
        return keys.at[step, pl.ds(h * HALF, HALF)]

    def bulk(index, src, step, h, device):
        return remote(S_BULK + index, src, key_half(step, h), bulk_sem.at[step, h], device)

    own = lambda h: half(stale_hbm, h)
    bulks = {
        "own0_r": bulk(0, own(0), 1, 0, right),
        "own1_l": bulk(1, own(1), 1, 1, left),
        "own1_r": bulk(2, own(1), 2, 0, right),
        "own0_l": bulk(3, own(0), 2, 1, left),
        "fwd0_r": bulk(4, key_half(1, 0), 3, 0, right),
        "fwd1_l": bulk(5, key_half(1, 1), 3, 1, left),
        "z0": bulk(6, own(0), 4, 0, partner),
        "z1": bulk(7, own(1), 4, 1, partner),
        "p0_r": bulk(8, key_half(4, 0), 5, 0, right),
        "p0_l": bulk(9, key_half(4, 0), 5, 1, left),
        "p1_r": bulk(10, key_half(4, 1), 6, 0, right),
        "p1_l": bulk(11, key_half(4, 1), 6, 1, left),
        "pf0_r": bulk(12, key_half(5, 0), 7, 0, right),
        "pf1_l": bulk(13, key_half(6, 1), 7, 1, left),
    }

    def wait_half(step, h):
        bulk(0, own(0), step, h, right).wait_recv()

    load[D_FEAT].wait()
    x = feats[pl.ds(ROW, TOK), :].astype(F32)
    mean = jnp.sum(x, axis=0, keepdims=True) * (1.0 / TOK)
    stats[0, 0:1, :] = mean
    stats[0, 1:2, :] = jnp.sum((x - mean) * (x - mean), axis=0, keepdims=True)
    stats[0, 2:8, :] = jnp.zeros((6, CH), F32)

    def stat(slot, src, dst, recv, device):
        return remote(slot, stats.at[src], stats.at[dst], recv_sem.at[recv], device)

    stat_r = stat(S_STAT_R, 0, 1, R_STAT_L, right)
    stat_l = stat(S_STAT_L, 0, 2, R_STAT_R, left)
    stat_o = stat(S_STAT_O, 1, 3, R_STAT_O, right)
    stat_p = stat(S_STAT_P, 4, 5, R_STAT_P, partner)
    halo_r = remote(S_HALO_R, feat_hbm.at[pl.ds(TOK - ROW, ROW)], feats.at[pl.ds(0, ROW)], recv_sem.at[R_TOP], right)
    halo_l = remote(S_HALO_L, feat_hbm.at[pl.ds(0, ROW)], feats.at[pl.ds(ROW + TOK, ROW)], recv_sem.at[R_BOTTOM], left)
    corner_top = remote(S_CORNER, feats.at[pl.ds(0, ROW)], corner, recv_sem.at[R_CORNER], partner)
    corner_bottom = remote(S_CORNER, feats.at[pl.ds(ROW + TOK, ROW)], corner, recv_sem.at[R_CORNER], partner)

    pl.semaphore_wait(barrier, 3)
    stat_r.start()
    stat_l.start()
    halo_r.start()
    halo_l.start()
    bulks["own0_r"].start()
    bulks["own1_l"].start()
    bulks["z0"].start()
    bulks["own1_r"].start()
    bulks["own0_l"].start()

    load[D_HID].wait()
    load[D_WQ].wait()
    query = jnp.dot(keys[0], wq[...], preferred_element_type=F32).astype(BF16).astype(F32) * 0.125
    zero = jnp.zeros((PAIR_CH // 2, TOK), BF16)
    for p in range(PAIRS):
        t = query[:, PAIR_CH * p : PAIR_CH * (p + 1)].T.astype(BF16)
        qt[p, 0:64, 0:TOK] = t[0:64]
        qt[p, 64:128, 0:TOK] = zero
        qt[p, 0:64, TOK:PAIR_Q] = zero
        qt[p, 64:128, TOK:PAIR_Q] = t[64:128]
        vt[p, PAIR_CH:VROWS, :] = jnp.ones((VROWS - PAIR_CH, TOK), BF16)
    load[D_WV].wait()
    wvt[...] = wv[...].astype(F32).T.astype(BF16)
    load[D_WK].wait()
    row_max[...] = jnp.full(row_max.shape, -1e30, F32)
    acc[...] = jnp.zeros(acc.shape, F32)

    def attend(step):
        source = keys[step]
        kbuf[...] = jnp.dot(source, wk[...], preferred_element_type=F32).astype(BF16)
        value = lax.dot_general(wvt[...], source, NT, preferred_element_type=F32).astype(BF16)
        for p in range(PAIRS):
            vt[p, 0:PAIR_CH, :] = value[PAIR_CH * p : PAIR_CH * (p + 1), :]

        def score(p):
            scores[p % 2] = jnp.dot(
                kbuf[:, PAIR_CH * p : PAIR_CH * (p + 1)], qt[p], preferred_element_type=F32
            )

        def soften(p):
            s = scores[p % 2]
            old = row_max[p]
            new = jnp.maximum(old, jnp.max(s, axis=0, keepdims=True))
            probs[p % 2] = jnp.exp(s - new).astype(BF16)
            row_max[p] = new
            return jnp.exp(old - new)

        def weigh(p, factor):
            acc[p] = acc[p] * factor + jnp.dot(vt[p], probs[p % 2], preferred_element_type=F32)

        score(0)
        factor = None
        for p in range(PAIRS + 1):
            if p + 1 < PAIRS:
                score(p + 1)
            if p >= 1:
                weigh(p - 1, factor)
            if p < PAIRS:
                factor = soften(p)

    attend(0)

    stat_r.wait_recv()
    stat_l.wait_recv()
    stat_o.start()


    halo_r.wait_recv()
    halo_l.wait_recv()

    @pl.when(me == 0)
    def _():
        corner_top.start()

    @pl.when(me == PATCHES - 1)
    def _():
        corner_bottom.start()

    stat_o.wait_recv()
    s4 = [stats[i] for i in range(4)]
    half_mean = (s4[0] + s4[1] + s4[2] + s4[3]) * 0.25
    half_dev = s4[0] + s4[1] + s4[2] + s4[3]
    spread = sum((s - half_mean) * (s - half_mean) for s in s4) * TOK
    stats[4, 0:1, :] = half_mean[0:1]
    stats[4, 1:2, :] = half_dev[1:2] + spread[0:1]
    stats[4, 2:8, :] = jnp.zeros((6, CH), F32)
    stat_p.start()

    @pl.when((me == RING - 1) | (me == RING))
    def _():
        corner_top.wait_recv()

    @pl.when(me == RING)
    def _():
        feats[pl.ds(0, ROW), :] = corner[...]

    @pl.when(me == RING - 1)
    def _():
        feats[pl.ds(ROW + TOK, ROW), :] = corner[...]

    stat_p.wait_recv()
    a, b = stats[4], stats[5]
    both_mean = (a + b) * 0.5
    channel_dev = (a + b)[1:2] + ((a - b) * (a - b))[0:1] * (TOK * RING * 0.5)
    channel = lax.broadcasted_iota(jnp.int32, (CH, ROW), 0)
    group = lax.broadcasted_iota(jnp.int32, (CH, ROW), 1) * GROUP_CH
    member = ((channel >= group) & (channel < group + GROUP_CH)).astype(F32)

    def over_group(v):
        total = jnp.dot(jnp.broadcast_to(v, (8, CH)), member, precision=HIGHEST, preferred_element_type=F32)
        return lax.dot_general(total, member, NT, precision=HIGHEST, preferred_element_type=F32)[0:1]

    group_mean = over_group(both_mean[0:1]) * (1.0 / GROUP_CH)
    off = both_mean[0:1] - group_mean
    tokens = TOK * PATCHES
    variance = over_group(channel_dev + off * off * tokens) * (1.0 / (GROUP_CH * tokens))
    scale = lax.rsqrt(variance + EPSILON)

    column = lax.broadcasted_iota(jnp.int32, (ROW, CH), 0)
    for r in range(5):
        v = feats[pl.ds(r * ROW, ROW), :].astype(F32)
        v = (v - group_mean) * scale * gain[...] + shift[...]
        v = v / (1.0 + jnp.exp(-v))
        if r == 0:
            v = jnp.where(me == 0, 0.0, v)
        if r == 4:
            v = jnp.where(me == PATCHES - 1, 0.0, v)
        act[pl.ds(r * ROW, ROW), 0:CH] = jnp.where(column == 0, 0.0, pltpu.roll(v, 1, 0)).astype(BF16)
        act[pl.ds(r * ROW, ROW), CH : 2 * CH] = v.astype(BF16)
        act[pl.ds(r * ROW, ROW), 2 * CH : 3 * CH] = jnp.where(
            column == ROW - 1, 0.0, pltpu.roll(v, ROW - 1, 0)
        ).astype(BF16)

    load[D_TW].wait()
    features_half = tw.shape[0] // 2
    j = lax.broadcasted_iota(jnp.int32, (16, features_half), 1).astype(F32)
    angle = timestep[0].astype(F32) * jnp.exp(j * (-math.log(10000.0) / features_half))
    cos, sin = jnp.cos(angle), jnp.sin(angle)
    cos = (cos / (1.0 + jnp.exp(-cos))).astype(BF16)
    sin = (sin / (1.0 + jnp.exp(-sin))).astype(BF16)
    time_shift = jnp.dot(cos, tw[0:features_half, :], preferred_element_type=F32) + jnp.dot(
        sin, tw[features_half:, :], preferred_element_type=F32
    )

    load[D_CONV].wait()
    conv_acc[...] = jnp.broadcast_to(time_shift[0:1], (TOK, CH))

    def conv_row(r, carry):
        conv_acc[...] += jnp.dot(
            act[pl.ds(pl.multiple_of(r * ROW, ROW), TOK), :], convw[r], preferred_element_type=F32
        )
        return carry

    lax.fori_loop(0, 3, conv_row, 0)
    res_ref[...] = conv_acc[...].astype(BF16)

    def stale_step(step, carry):
        @pl.when(step == 3)
        def _():
            wait_half(4, 0)
            bulks["p0_r"].start()
            bulks["p0_l"].start()

        @pl.when(step != 4)
        def _():
            wait_half(step, 0)

        wait_half(step, 1)

        @pl.when(step == 1)
        def _():
            bulks["fwd0_r"].start()
            bulks["fwd1_l"].start()
            bulks["z0"].wait_send()
            bulks["z1"].start()

        @pl.when(step == 4)
        def _():
            bulks["p1_r"].start()
            bulks["p1_l"].start()

        @pl.when(step == 5)
        def _():
            bulks["pf0_r"].start()

        @pl.when(step == 6)
        def _():
            bulks["pf1_l"].start()

        attend(step)
        return carry

    lax.fori_loop(1, PATCHES, stale_step, 0)

    for p in range(PAIRS):
        total = acc[p]
        first = total[0:64, 0:TOK] / total[PAIR_CH : PAIR_CH + 1, 0:TOK]
        second = total[64:128, TOK:PAIR_Q] / total[PAIR_CH : PAIR_CH + 1, TOK:PAIR_Q]
        attn_ref[:, PAIR_CH * p : PAIR_CH * (p + 1)] = jnp.concatenate([first, second], axis=0).T.astype(BF16)

    for copy in (stat_r, stat_l, stat_o, stat_p, halo_r, halo_l):
        copy.wait_send()
    for name, copy in bulks.items():
        if name != "z0":
            copy.wait_send()

    @pl.when((me == 0) | (me == PATCHES - 1))
    def _():
        corner_top.wait_send()


def per_device(timestep, features, hidden, stale_hidden, gn_gain, gn_shift, conv_kernel, time_weight, wq, wk, wv):
    anywhere = pl.BlockSpec(memory_space=pl.ANY)
    vmem = pl.BlockSpec(memory_space=pltpu.VMEM)
    smem = pl.BlockSpec(memory_space=pltpu.SMEM)
    out = jax.ShapeDtypeStruct((TOK, CH), BF16)
    return pl.pallas_call(
        kernel,
        out_shape=(out, out),
        in_specs=[smem, anywhere, anywhere, anywhere, vmem, vmem] + [anywhere] * 5,
        out_specs=(vmem, vmem),
        scratch_shapes=[
            pltpu.VMEM((PATCHES, TOK, CH), BF16),
            pltpu.VMEM((TOK + 2 * ROW, CH), BF16),
            pltpu.VMEM((ROW, CH), BF16),
            pltpu.VMEM((6, 8, CH), F32),
            pltpu.VMEM((CH, CH), BF16),
            pltpu.VMEM((CH, CH), BF16),
            pltpu.VMEM((CH, CH), BF16),
            pltpu.VMEM((CH, CH), BF16),
            pltpu.VMEM((320, CH), BF16),
            pltpu.VMEM((3, 3 * CH, CH), BF16),
            pltpu.VMEM((TOK + 2 * ROW, 3 * CH), BF16),
            pltpu.VMEM((PAIRS, PAIR_CH, PAIR_Q), BF16),
            pltpu.VMEM((TOK, CH), BF16),
            pltpu.VMEM((PAIRS, VROWS, TOK), BF16),
            pltpu.VMEM((2, TOK, PAIR_Q), F32),
            pltpu.VMEM((2, TOK, PAIR_Q), BF16),
            pltpu.VMEM((PAIRS, 1, PAIR_Q), F32),
            pltpu.VMEM((PAIRS, VROWS, PAIR_Q), F32),
            pltpu.VMEM((TOK, CH), F32),
            pltpu.SemaphoreType.DMA((N_SENDS,)),
            pltpu.SemaphoreType.DMA((7,)),
            pltpu.SemaphoreType.DMA((PATCHES, 2)),
            pltpu.SemaphoreType.DMA((7,)),
        ],
        compiler_params=pltpu.CompilerParams(
            collective_id=0, has_side_effects=True, vmem_limit_bytes=56 * 2**20
        ),
    )(
        timestep, features, hidden, stale_hidden, gn_gain.reshape(1, CH), gn_shift.reshape(1, CH),
        conv_kernel.reshape(3, 3 * CH, CH), time_weight, wq, wk, wv,
    )


def solution(mesh):
    tokens = P(("batch", "patch"), None)
    return jax.shard_map(
        per_device,
        mesh=mesh,
        in_specs=(P("batch"), tokens, tokens, tokens) + (P(),) * 7,
        out_specs=(tokens, tokens),
        check_vma=False,
    )
```

```python
import functools
import math

import jax
import jax.numpy as jnp
from jax import lax
from jax.experimental import pallas as pl
from jax.experimental.pallas import tpu as pltpu
from jax.sharding import PartitionSpec as P

F32, BF16 = jnp.float32, jnp.bfloat16
MESH = pl.DeviceIdType.MESH
NT = (((1,), (1,)), ((), ()))
HIGHEST = lax.Precision.HIGHEST
TOK, CH, ROW, HALF, QUARTER, EIGHTH = 384, 640, 128, 192, 96, 48
GROUPS, GROUP_CH, PATCHES, RING = 16, 40, 8, 4
PAIRS, PAIR_CH, PAIR_Q = 5, 128, 768
VROWS = 144
EPSILON = 1e-05
S_STAT_R, S_STAT_L, S_STAT_O, S_STAT_P, S_DOWN, S_UP = range(6)
S_BULK = 6
N_SENDS = S_BULK + 22
R_STAT_L, R_STAT_R, R_STAT_O, R_STAT_P, R_TOP, R_BOTTOM = range(6)
D_FEAT, D_HID, D_WQ, D_WK, D_WV, D_TW, D_CONV, D_GAIN, D_SHIFT, D_STEP = range(10)


def kernel(
    step_hbm, feat_hbm, hid_hbm, stale_hbm, gain_hbm, shift_hbm, conv_hbm, tw_hbm, wq_hbm, wk_hbm, wv_hbm,
    res_ref, attn_ref,
    keys, feats, stats, wq, wk, wv, wvt, tw, convw, act, qt, kbuf, vt, scores, probs,
    row_max, acc, conv_acc, gain, shift, timestep, send_sem, recv_sem, bulk_sem, load_sem, late_sem, seam_sem,
):
    me = lax.axis_index("patch")
    y, zh = lax.rem(me, RING), lax.div(me, RING)
    right = {"patch": zh * RING + lax.rem(y + 1, RING)}
    left = {"patch": zh * RING + lax.rem(y + RING - 1, RING)}
    across = {"patch": zh * RING + lax.rem(y + 2, RING)}
    partner = {"patch": (1 - zh) * RING + y}

    barrier = pltpu.get_barrier_semaphore()
    for device in (right, left, across):
        pl.semaphore_signal(barrier, inc=1, device_id=device, device_id_type=MESH)

    @pl.when(zh == 0)
    def _():
        pl.semaphore_signal(barrier, inc=1, device_id=partner, device_id_type=MESH)

    @pl.when(me == RING - 1)
    def _():
        pl.semaphore_signal(barrier, inc=1, device_id={"patch": me + 1}, device_id_type=MESH)

    loads = [
        (D_FEAT, feat_hbm, feats.at[pl.ds(ROW, TOK)]),
        (D_HID, hid_hbm, keys.at[0]),
        (D_WQ, wq_hbm, wq),
        (D_WK, wk_hbm, wk),
        (D_WV, wv_hbm, wv),
        (D_TW, tw_hbm, tw),
        (D_CONV, conv_hbm, convw),
        (D_GAIN, gain_hbm, gain),
        (D_SHIFT, shift_hbm, shift),
        (D_STEP, step_hbm, timestep),
    ]
    load = {i: pltpu.make_async_copy(src, dst, load_sem.at[i]) for i, src, dst in loads}
    for i, _, _ in loads:
        if i != D_CONV:
            load[i].start()

    def remote(slot, src, dst, recv, device):
        return pltpu.make_async_remote_copy(
            src_ref=src, dst_ref=dst, send_sem=send_sem.at[slot], recv_sem=recv,
            device_id=device, device_id_type=MESH,
        )

    def rows(step, first, count):
        return keys.at[step, pl.ds(first, count)]

    def bulk(index, src, step, first, count, device):
        return remote(
            S_BULK + index, src, rows(step, first, count), bulk_sem.at[step, first // EIGHTH], device
        )

    def own(first, count):
        return stale_hbm.at[pl.ds(first, count)]

    moves = {
        "r0": (own(0, HALF), 1, 0, HALF, right),
        "l1": (own(HALF, HALF), 1, HALF, HALF, left),
        "r1": (own(HALF, HALF), 2, 0, HALF, right),
        "l0": (own(0, HALF), 2, HALF, HALF, left),
        "or": (rows(1, 0, HALF), 3, 0, HALF, right),
        "ol": (rows(1, HALF, HALF), 3, HALF, HALF, left),
        "z0": (own(0, QUARTER), 5, 0, QUARTER, partner),
        "z1": (own(QUARTER, QUARTER), 5, QUARTER, QUARTER, partner),
        "z2": (own(HALF, QUARTER), 5, HALF, QUARTER, partner),
        "z3": (own(HALF + QUARTER, QUARTER), 5, HALF + QUARTER, QUARTER, partner),
        "pr0": (rows(5, 0, HALF), 4, 0, HALF, right),
        "pl0": (rows(5, 0, HALF), 4, HALF, HALF, left),
        "pr2": (rows(5, HALF, QUARTER), 6, HALF, QUARTER, right),
        "pl2": (rows(5, HALF, QUARTER), 6, HALF + QUARTER, QUARTER, left),
        "pr3": (rows(5, HALF + QUARTER, QUARTER), 7, 0, QUARTER, right),
        "pl3": (rows(5, HALF + QUARTER, QUARTER), 7, QUARTER, QUARTER, left),
        "po0": (rows(4, 0, QUARTER), 6, 0, QUARTER, right),
        "po1": (rows(4, HALF + QUARTER, QUARTER), 6, QUARTER, QUARTER, left),
        "po2": (rows(6, HALF, QUARTER), 7, HALF, QUARTER, right),
        "oz": (rows(3, HALF + QUARTER, QUARTER), 7, HALF + QUARTER, QUARTER, partner),
    }
    bulks = {name: bulk(i, *move) for i, (name, move) in enumerate(moves.items())}

    def go(*names):
        for name in names:
            bulks[name].start()

    def got(*names):
        for name in names:
            bulks[name].wait_recv()

    def stat(slot, src, dst, recv, device):
        return remote(slot, stats.at[src], stats.at[dst], recv_sem.at[recv], device)

    stat_r = stat(S_STAT_R, 0, 1, R_STAT_L, right)
    stat_l = stat(S_STAT_L, 0, 2, R_STAT_R, left)
    stat_o = stat(S_STAT_O, 0, 3, R_STAT_O, across)
    stat_p = stat(S_STAT_P, 4, 5, R_STAT_P, partner)
    down = remote(S_DOWN, feat_hbm.at[pl.ds(TOK - ROW, ROW)], feats.at[pl.ds(0, ROW)], recv_sem.at[R_TOP], {"patch": me + 1})
    up = remote(S_UP, feat_hbm.at[pl.ds(0, ROW)], feats.at[pl.ds(ROW + TOK, ROW)], recv_sem.at[R_BOTTOM], {"patch": me - 1})

    @pl.when(me == 0)
    def _():
        feats[pl.ds(0, ROW), :] = jnp.zeros((ROW, CH), BF16)

    @pl.when(me == PATCHES - 1)
    def _():
        feats[pl.ds(ROW + TOK, ROW), :] = jnp.zeros((ROW, CH), BF16)

    def local_stats():
        load[D_FEAT].wait()
        x = feats[pl.ds(ROW, TOK), :].astype(F32)
        mean = jnp.sum(x, axis=0, keepdims=True) * (1.0 / TOK)
        stats[0, 0:1, :] = mean
        stats[0, 1:2, :] = jnp.sum((x - mean) * (x - mean), axis=0, keepdims=True)
        stats[0, 2:8, :] = jnp.zeros((6, CH), F32)

    def prepare():
        load[D_HID].wait()
        load[D_WQ].wait()
        query = jnp.dot(keys[0], wq[...], preferred_element_type=F32).astype(BF16).astype(F32) * 0.125
        zero = jnp.zeros((PAIR_CH // 2, TOK), BF16)
        for p in range(PAIRS):
            t = query[:, PAIR_CH * p : PAIR_CH * (p + 1)].T.astype(BF16)
            qt[p, 0:64, 0:TOK] = t[0:64]
            qt[p, 64:128, 0:TOK] = zero
            qt[p, 0:64, TOK:PAIR_Q] = zero
            qt[p, 64:128, TOK:PAIR_Q] = t[64:128]
            vt[p, PAIR_CH:VROWS, :] = jnp.ones((VROWS - PAIR_CH, TOK), BF16)
        load[D_WV].wait()
        wvt[...] = wv[...].astype(F32).T.astype(BF16)
        load[D_WK].wait()
        row_max[...] = jnp.full(row_max.shape, -1e30, F32)
        acc[...] = jnp.zeros(acc.shape, F32)

    def open_ring():
        @pl.when(zh == 0)
        def _():
            pl.semaphore_wait(barrier, 3)

        @pl.when((zh == 1) & (me != RING))
        def _():
            pl.semaphore_wait(barrier, 4)

        @pl.when(me == RING)
        def _():
            pl.semaphore_wait(barrier, 5)

        stat_r.start()
        stat_l.start()
        stat_o.start()
        go("r0", "l1")

        @pl.when(me == RING)
        def _():
            pl.semaphore_signal(seam_sem, inc=1, device_id={"patch": me - 1}, device_id_type=MESH)
            up.start()

        @pl.when(zh == 1)
        def _():
            pl.semaphore_signal(late_sem, inc=1, device_id=partner, device_id_type=MESH)
            go("z0")

        go("r1", "l0")

        @pl.when((me != RING - 1) & (me < PATCHES - 1))
        def _():
            down.start()

        @pl.when((me != RING) & (me > 0))
        def _():
            up.start()

    early = (zh == 0) & (y < 2)
    local_stats()

    @pl.when(early)
    def _():
        prepare()

    open_ring()

    @pl.when(jnp.logical_not(early))
    def _():
        prepare()

    load[D_CONV].start()

    def attend(step):
        source = keys[step]
        kbuf[...] = jnp.dot(source, wk[...], preferred_element_type=F32).astype(BF16)
        value = lax.dot_general(wvt[...], source, NT, preferred_element_type=F32).astype(BF16)
        for p in range(PAIRS):
            vt[p, 0:PAIR_CH, :] = value[PAIR_CH * p : PAIR_CH * (p + 1), :]

        def score(p):
            scores[p % 2] = jnp.dot(
                kbuf[:, PAIR_CH * p : PAIR_CH * (p + 1)], qt[p], preferred_element_type=F32
            )

        def soften(p):
            s = scores[p % 2]
            old = row_max[p]
            new = jnp.maximum(old, jnp.max(s, axis=0, keepdims=True))
            probs[p % 2] = jnp.exp(s - new).astype(BF16)
            row_max[p] = new
            return jnp.exp(old - new)

        def weigh(p, factor):
            acc[p] = acc[p] * factor + jnp.dot(vt[p], probs[p % 2], preferred_element_type=F32)

        score(0)
        factor = None
        for p in range(PAIRS + 1):
            if p + 1 < PAIRS:
                score(p + 1)
            if p >= 1:
                weigh(p - 1, factor)
            if p < PAIRS:
                factor = soften(p)

    def combine_ring():
        stat_r.wait_recv()
        stat_l.wait_recv()
        stat_o.wait_recv()
        s4 = [stats[i] for i in range(4)]
        half_mean = (s4[0] + s4[1] + s4[2] + s4[3]) * 0.25
        half_dev = s4[0] + s4[1] + s4[2] + s4[3]
        spread = sum((s - half_mean) * (s - half_mean) for s in s4) * TOK
        stats[4, 0:1, :] = half_mean[0:1]
        stats[4, 1:2, :] = half_dev[1:2] + spread[0:1]
        stats[4, 2:8, :] = jnp.zeros((6, CH), F32)

    def resnet():
        @pl.when(me > 0)
        def _():
            down.wait_recv()

        @pl.when(me < PATCHES - 1)
        def _():
            up.wait_recv()

        stat_p.wait_recv()
        a, b = stats[4], stats[5]
        both_mean = (a + b) * 0.5
        channel_dev = (a + b)[1:2] + ((a - b) * (a - b))[0:1] * (TOK * RING * 0.5)
        channel = lax.broadcasted_iota(jnp.int32, (CH, ROW), 0)
        group = lax.broadcasted_iota(jnp.int32, (CH, ROW), 1) * GROUP_CH
        member = ((channel >= group) & (channel < group + GROUP_CH)).astype(F32)

        def over_group(v):
            total = jnp.dot(jnp.broadcast_to(v, (8, CH)), member, precision=HIGHEST, preferred_element_type=F32)
            return lax.dot_general(total, member, NT, precision=HIGHEST, preferred_element_type=F32)[0:1]

        group_mean = over_group(both_mean[0:1]) * (1.0 / GROUP_CH)
        off = both_mean[0:1] - group_mean
        tokens = TOK * PATCHES
        variance = over_group(channel_dev + off * off * tokens) * (1.0 / (GROUP_CH * tokens))
        scale = lax.rsqrt(variance + EPSILON)

        load[D_GAIN].wait()
        load[D_SHIFT].wait()
        gain_row, shift_row = gain[...].reshape(1, CH), shift[...].reshape(1, CH)
        column = lax.broadcasted_iota(jnp.int32, (ROW, CH), 0)
        for r in range(5):
            v = feats[pl.ds(r * ROW, ROW), :].astype(F32)
            v = (v - group_mean) * scale * gain_row + shift_row
            v = v / (1.0 + jnp.exp(-v))
            if r == 0:
                v = jnp.where(me == 0, 0.0, v)
            if r == 4:
                v = jnp.where(me == PATCHES - 1, 0.0, v)
            act[pl.ds(r * ROW, ROW), 0:CH] = jnp.where(column == 0, 0.0, pltpu.roll(v, 1, 0)).astype(BF16)
            act[pl.ds(r * ROW, ROW), CH : 2 * CH] = v.astype(BF16)
            act[pl.ds(r * ROW, ROW), 2 * CH : 3 * CH] = jnp.where(
                column == ROW - 1, 0.0, pltpu.roll(v, ROW - 1, 0)
            ).astype(BF16)

        load[D_TW].wait()
        load[D_STEP].wait()
        features_half = tw.shape[0] // 2
        j = lax.broadcasted_iota(jnp.int32, (16, features_half), 1).astype(F32)
        angle = timestep[0].astype(F32) * jnp.exp(j * (-math.log(10000.0) / features_half))
        cos, sin = jnp.cos(angle), jnp.sin(angle)
        cos = (cos / (1.0 + jnp.exp(-cos))).astype(BF16)
        sin = (sin / (1.0 + jnp.exp(-sin))).astype(BF16)
        time_shift = jnp.dot(cos, tw[0:features_half, :], preferred_element_type=F32) + jnp.dot(
            sin, tw[features_half:, :], preferred_element_type=F32
        )

        load[D_CONV].wait()
        conv_acc[...] = jnp.broadcast_to(time_shift[0:1], (TOK, CH))

        def conv_row(r, carry):
            conv_acc[...] += jnp.dot(
                act[pl.ds(pl.multiple_of(r * ROW, ROW), TOK), :], convw[r], preferred_element_type=F32
            )
            return carry

        conv_row(0, 0)
        got("z0", "z1")
        go("pr0", "pl0")
        lax.fori_loop(1, 3, conv_row, 0)
        res_ref[...] = conv_acc[...].astype(BF16)


    def one_step(step, carry):
        @pl.when(step == 1)
        def _():
            combine_ring()

            @pl.when(zh == 0)
            def _():
                pl.semaphore_wait(late_sem, 1)

            stat_p.start()

            @pl.when(me == RING - 1)
            def _():
                pl.semaphore_wait(seam_sem, 1)
                down.start()

            @pl.when(zh == 0)
            def _():
                go("z0")

            go("z1", "z2", "z3")
            got("r0", "l1")
            go("or", "ol")

        @pl.when(step == 2)
        def _():
            got("r1", "l0")

        @pl.when(step == 3)
        def _():
            resnet()
            got("or", "ol")
            go("oz")

        @pl.when(step == 4)
        def _():
            got("z2")
            go("pr2", "pl2")
            got("pr0", "pl0")
            go("po0", "po1")

        @pl.when(step == 5)
        def _():
            got("z3")
            go("pr3", "pl3")
            got("pr2")
            go("po2")

        @pl.when(step == 6)
        def _():
            got("pl2", "po0", "po1")

        @pl.when(step == 7)
        def _():
            got("pr3", "pl3", "po2", "oz")

        attend(step)
        return carry

    lax.fori_loop(0, PATCHES, one_step, 0)

    for p in range(PAIRS):
        total = acc[p]
        first = total[0:64, 0:TOK] / total[PAIR_CH : PAIR_CH + 1, 0:TOK]
        second = total[64:128, TOK:PAIR_Q] / total[PAIR_CH : PAIR_CH + 1, TOK:PAIR_Q]
        attn_ref[:, PAIR_CH * p : PAIR_CH * (p + 1)] = jnp.concatenate([first, second], axis=0).T.astype(BF16)

    for copy in (stat_r, stat_l, stat_o, stat_p):
        copy.wait_send()

    @pl.when(me < PATCHES - 1)
    def _():
        down.wait_send()

    @pl.when(me > 0)
    def _():
        up.wait_send()

    for copy in bulks.values():
        copy.wait_send()


def per_device(timestep, features, hidden, stale_hidden, gn_gain, gn_shift, conv_kernel, time_weight, wq, wk, wv):
    anywhere = pl.BlockSpec(memory_space=pl.ANY)
    vmem = pl.BlockSpec(memory_space=pltpu.VMEM)
    out = jax.ShapeDtypeStruct((TOK, CH), BF16)
    return pl.pallas_call(
        kernel,
        out_shape=(out, out),
        in_specs=[anywhere] * 11,
        out_specs=(vmem, vmem),
        scratch_shapes=[
            pltpu.VMEM((PATCHES, TOK, CH), BF16),
            pltpu.VMEM((TOK + 2 * ROW, CH), BF16),
            pltpu.VMEM((6, 8, CH), F32),
            pltpu.VMEM((CH, CH), BF16),
            pltpu.VMEM((CH, CH), BF16),
            pltpu.VMEM((CH, CH), BF16),
            pltpu.VMEM((CH, CH), BF16),
            pltpu.VMEM((320, CH), BF16),
            pltpu.VMEM((3, 3 * CH, CH), BF16),
            pltpu.VMEM((TOK + 2 * ROW, 3 * CH), BF16),
            pltpu.VMEM((PAIRS, PAIR_CH, PAIR_Q), BF16),
            pltpu.VMEM((TOK, CH), BF16),
            pltpu.VMEM((PAIRS, VROWS, TOK), BF16),
            pltpu.VMEM((2, TOK, PAIR_Q), F32),
            pltpu.VMEM((2, TOK, PAIR_Q), BF16),
            pltpu.VMEM((PAIRS, 1, PAIR_Q), F32),
            pltpu.VMEM((PAIRS, VROWS, PAIR_Q), F32),
            pltpu.VMEM((TOK, CH), F32),
            pltpu.VMEM((CH,), F32),
            pltpu.VMEM((CH,), F32),
            pltpu.SMEM((1,), jnp.int32),
            pltpu.SemaphoreType.DMA((N_SENDS,)),
            pltpu.SemaphoreType.DMA((6,)),
            pltpu.SemaphoreType.DMA((PATCHES, 8)),
            pltpu.SemaphoreType.DMA((10,)),
            pltpu.SemaphoreType.REGULAR,
            pltpu.SemaphoreType.REGULAR,
        ],
        compiler_params=pltpu.CompilerParams(
            collective_id=0, has_side_effects=True, vmem_limit_bytes=56 * 2**20
        ),
    )(
        timestep, features, hidden, stale_hidden, gn_gain, gn_shift,
        conv_kernel.reshape(3, 3 * CH, CH), time_weight, wq, wk, wv,
    )


def solution(mesh):
    tokens = P(("batch", "patch"), None)
    return jax.shard_map(
        per_device,
        mesh=mesh,
        in_specs=(P("batch"), tokens, tokens, tokens) + (P(),) * 7,
        out_specs=(tokens, tokens),
        check_vma=False,
    )
```

```python
import functools
import math

import jax
import jax.numpy as jnp
from jax import lax
from jax.experimental import pallas as pl
from jax.experimental.pallas import tpu as pltpu
from jax.sharding import PartitionSpec as P

F32, BF16 = jnp.float32, jnp.bfloat16
MESH = pl.DeviceIdType.MESH
NT = (((1,), (1,)), ((), ()))
HIGHEST = lax.Precision.HIGHEST
TOK, CH, ROW, HALF, QUARTER, EIGHTH = 384, 640, 128, 192, 96, 48
GROUPS, GROUP_CH, PATCHES, RING = 16, 40, 8, 4
PAIRS, PAIR_CH, PAIR_Q = 5, 128, 768
VROWS = 144
EPSILON = 1e-05
S_STAT_R, S_STAT_L, S_STAT_O, S_STAT_P, S_DOWN, S_UP = range(6)
S_BULK = 6
N_SENDS = S_BULK + 22
R_STAT_L, R_STAT_R, R_STAT_O, R_STAT_P, R_TOP, R_BOTTOM = range(6)
D_FEAT, D_HID, D_WQ, D_WK, D_WV, D_TW, D_CONV, D_GAIN, D_SHIFT, D_STEP = range(10)


def kernel(
    step_hbm, feat_hbm, hid_hbm, stale_hbm, gain_hbm, shift_hbm, conv_hbm, tw_hbm, wq_hbm, wk_hbm, wv_hbm,
    res_ref, attn_ref,
    keys, feats, stats, wq, wk, wv, wvt, tw, convw, act, qt, kbuf, vt, scores, probs,
    row_max, acc, conv_acc, norm, gain, shift, timestep, send_sem, recv_sem, bulk_sem, load_sem, late_sem, seam_sem,
):
    me = lax.axis_index("patch")
    y, zh = lax.rem(me, RING), lax.div(me, RING)
    right = {"patch": zh * RING + lax.rem(y + 1, RING)}
    left = {"patch": zh * RING + lax.rem(y + RING - 1, RING)}
    across = {"patch": zh * RING + lax.rem(y + 2, RING)}
    partner = {"patch": (1 - zh) * RING + y}

    barrier = pltpu.get_barrier_semaphore()
    for device in (right, left, across):
        pl.semaphore_signal(barrier, inc=1, device_id=device, device_id_type=MESH)

    @pl.when(zh == 0)
    def _():
        pl.semaphore_signal(barrier, inc=1, device_id=partner, device_id_type=MESH)

    @pl.when(me == RING - 1)
    def _():
        pl.semaphore_signal(barrier, inc=1, device_id={"patch": me + 1}, device_id_type=MESH)

    loads = [
        (D_FEAT, feat_hbm, feats.at[pl.ds(ROW, TOK)]),
        (D_HID, hid_hbm, keys.at[0]),
        (D_WQ, wq_hbm, wq),
        (D_WK, wk_hbm, wk),
        (D_WV, wv_hbm, wv),
        (D_TW, tw_hbm, tw),
        (D_CONV, conv_hbm, convw),
        (D_GAIN, gain_hbm, gain),
        (D_SHIFT, shift_hbm, shift),
        (D_STEP, step_hbm, timestep),
    ]
    load = {i: pltpu.make_async_copy(src, dst, load_sem.at[i]) for i, src, dst in loads}
    for i, _, _ in loads:
        if i != D_CONV:
            load[i].start()

    def remote(slot, src, dst, recv, device):
        return pltpu.make_async_remote_copy(
            src_ref=src, dst_ref=dst, send_sem=send_sem.at[slot], recv_sem=recv,
            device_id=device, device_id_type=MESH,
        )

    def rows(step, first, count):
        return keys.at[step, pl.ds(first, count)]

    def bulk(index, src, step, first, count, device):
        return remote(
            S_BULK + index, src, rows(step, first, count), bulk_sem.at[step, first // EIGHTH], device
        )

    def own(first, count):
        return stale_hbm.at[pl.ds(first, count)]

    moves = {
        "r0": (own(0, HALF), 1, 0, HALF, right),
        "l1": (own(HALF, HALF), 1, HALF, HALF, left),
        "r1": (own(HALF, HALF), 2, 0, HALF, right),
        "l0": (own(0, HALF), 2, HALF, HALF, left),
        "or": (rows(1, 0, HALF), 3, 0, HALF, right),
        "ol": (rows(1, HALF, HALF), 3, HALF, HALF, left),
        "z0": (own(0, QUARTER), 5, 0, QUARTER, partner),
        "z1": (own(QUARTER, QUARTER), 5, QUARTER, QUARTER, partner),
        "z2": (own(HALF, QUARTER), 5, HALF, QUARTER, partner),
        "z3": (own(HALF + QUARTER, QUARTER), 5, HALF + QUARTER, QUARTER, partner),
        "pr0": (rows(5, 0, HALF), 4, 0, HALF, right),
        "pl0": (rows(5, 0, HALF), 4, HALF, HALF, left),
        "pr2": (rows(5, HALF, QUARTER), 6, HALF, QUARTER, right),
        "pl2": (rows(5, HALF, QUARTER), 6, HALF + QUARTER, QUARTER, left),
        "pr3": (rows(5, HALF + QUARTER, QUARTER), 7, 0, QUARTER, right),
        "pl3": (rows(5, HALF + QUARTER, QUARTER), 7, QUARTER, QUARTER, left),
        "po0": (rows(4, 0, QUARTER), 6, 0, QUARTER, right),
        "po1": (rows(4, HALF + QUARTER, QUARTER), 6, QUARTER, QUARTER, left),
        "po2": (rows(6, HALF, QUARTER), 7, HALF, QUARTER, right),
        "oz": (rows(3, HALF + QUARTER, QUARTER), 7, HALF + QUARTER, QUARTER, partner),
    }
    bulks = {name: bulk(i, *move) for i, (name, move) in enumerate(moves.items())}

    def go(*names):
        for name in names:
            bulks[name].start()

    def got(*names):
        for name in names:
            bulks[name].wait_recv()

    def stat(slot, src, dst, recv, device):
        return remote(slot, stats.at[src], stats.at[dst], recv_sem.at[recv], device)

    stat_r = stat(S_STAT_R, 0, 1, R_STAT_L, right)
    stat_l = stat(S_STAT_L, 0, 2, R_STAT_R, left)
    stat_o = stat(S_STAT_O, 0, 3, R_STAT_O, across)
    stat_p = stat(S_STAT_P, 4, 5, R_STAT_P, partner)
    down = remote(S_DOWN, feat_hbm.at[pl.ds(TOK - ROW, ROW)], feats.at[pl.ds(0, ROW)], recv_sem.at[R_TOP], {"patch": me + 1})
    up = remote(S_UP, feat_hbm.at[pl.ds(0, ROW)], feats.at[pl.ds(ROW + TOK, ROW)], recv_sem.at[R_BOTTOM], {"patch": me - 1})

    @pl.when(me == 0)
    def _():
        feats[pl.ds(0, ROW), :] = jnp.zeros((ROW, CH), BF16)

    @pl.when(me == PATCHES - 1)
    def _():
        feats[pl.ds(ROW + TOK, ROW), :] = jnp.zeros((ROW, CH), BF16)

    def local_stats():
        load[D_FEAT].wait()
        x = feats[pl.ds(ROW, TOK), :].astype(F32)
        mean = jnp.sum(x, axis=0, keepdims=True) * (1.0 / TOK)
        stats[0, 0:1, :] = mean
        stats[0, 1:2, :] = jnp.sum((x - mean) * (x - mean), axis=0, keepdims=True)
        stats[0, 2:8, :] = jnp.zeros((6, CH), F32)

    def prepare():
        load[D_HID].wait()
        load[D_WQ].wait()
        query = jnp.dot(keys[0], wq[...], preferred_element_type=F32).astype(BF16).astype(F32) * 0.125
        zero = jnp.zeros((PAIR_CH // 2, TOK), BF16)
        for p in range(PAIRS):
            t = query[:, PAIR_CH * p : PAIR_CH * (p + 1)].T.astype(BF16)
            qt[p, 0:64, 0:TOK] = t[0:64]
            qt[p, 64:128, 0:TOK] = zero
            qt[p, 0:64, TOK:PAIR_Q] = zero
            qt[p, 64:128, TOK:PAIR_Q] = t[64:128]
            vt[p, PAIR_CH:VROWS, :] = jnp.ones((VROWS - PAIR_CH, TOK), BF16)
        load[D_WV].wait()
        wvt[...] = wv[...].astype(F32).T.astype(BF16)
        load[D_WK].wait()
        row_max[...] = jnp.full(row_max.shape, -1e30, F32)
        acc[...] = jnp.zeros(acc.shape, F32)

    def open_ring():
        @pl.when(zh == 0)
        def _():
            pl.semaphore_wait(barrier, 3)

        @pl.when((zh == 1) & (me != RING))
        def _():
            pl.semaphore_wait(barrier, 4)

        @pl.when(me == RING)
        def _():
            pl.semaphore_wait(barrier, 5)

        stat_r.start()
        stat_l.start()
        stat_o.start()
        go("r0", "l1")

        @pl.when(me == RING)
        def _():
            pl.semaphore_signal(seam_sem, inc=1, device_id={"patch": me - 1}, device_id_type=MESH)

        @pl.when(zh == 1)
        def _():
            pl.semaphore_signal(late_sem, inc=1, device_id=partner, device_id_type=MESH)
            go("z0")

        go("r1", "l0")


    early = (zh == 0) & (y < 2)
    local_stats()

    @pl.when(early)
    def _():
        prepare()

    open_ring()

    @pl.when(jnp.logical_not(early))
    def _():
        prepare()

    load[D_CONV].start()

    def attend(step):
        source = keys[step]
        kbuf[...] = jnp.dot(source, wk[...], preferred_element_type=F32).astype(BF16)
        value = lax.dot_general(wvt[...], source, NT, preferred_element_type=F32).astype(BF16)
        for p in range(PAIRS):
            vt[p, 0:PAIR_CH, :] = value[PAIR_CH * p : PAIR_CH * (p + 1), :]

        def score(p):
            scores[p % 2] = jnp.dot(
                kbuf[:, PAIR_CH * p : PAIR_CH * (p + 1)], qt[p], preferred_element_type=F32
            )

        def soften(p):
            s = scores[p % 2]
            old = row_max[p]
            new = jnp.maximum(old, jnp.max(s, axis=0, keepdims=True))
            probs[p % 2] = jnp.exp(s - new).astype(BF16)
            row_max[p] = new
            return jnp.exp(old - new)

        def weigh(p, factor):
            acc[p] = acc[p] * factor + jnp.dot(vt[p], probs[p % 2], preferred_element_type=F32)

        score(0)
        factor = None
        for p in range(PAIRS + 1):
            if p + 1 < PAIRS:
                score(p + 1)
            if p >= 1:
                weigh(p - 1, factor)
            if p < PAIRS:
                factor = soften(p)

    def combine_ring():
        stat_r.wait_recv()
        stat_l.wait_recv()
        stat_o.wait_recv()
        s4 = [stats[i] for i in range(4)]
        half_mean = (s4[0] + s4[1] + s4[2] + s4[3]) * 0.25
        half_dev = s4[0] + s4[1] + s4[2] + s4[3]
        spread = sum((s - half_mean) * (s - half_mean) for s in s4) * TOK
        stats[4, 0:1, :] = half_mean[0:1]
        stats[4, 1:2, :] = half_dev[1:2] + spread[0:1]
        stats[4, 2:8, :] = jnp.zeros((6, CH), F32)

    def activate(r):
        group_mean, scale, gain_row, shift_row = affine_rows()
        column = lax.broadcasted_iota(jnp.int32, (ROW, CH), 0)
        v = feats[pl.ds(r * ROW, ROW), :].astype(F32)
        v = (v - group_mean) * scale * gain_row + shift_row
        v = v / (1.0 + jnp.exp(-v))
        if r == 0:
            v = jnp.where(me == 0, 0.0, v)
        if r == 4:
            v = jnp.where(me == PATCHES - 1, 0.0, v)
        act[pl.ds(r * ROW, ROW), 0:CH] = jnp.where(column == 0, 0.0, pltpu.roll(v, 1, 0)).astype(BF16)
        act[pl.ds(r * ROW, ROW), CH : 2 * CH] = v.astype(BF16)
        act[pl.ds(r * ROW, ROW), 2 * CH : 3 * CH] = jnp.where(
            column == ROW - 1, 0.0, pltpu.roll(v, ROW - 1, 0)
        ).astype(BF16)

    def affine_rows():
        return norm[0:1, :], norm[1:2, :], norm[2:3, :], norm[3:4, :]

    def convolve(first_row, first_out, count, tap):
        conv_acc[pl.ds(first_out, count), :] += jnp.dot(
            act[pl.ds(first_row, count), :], convw[tap], preferred_element_type=F32
        )

    def inner_rows():
        stat_p.wait_recv()
        a, b = stats[4], stats[5]
        both_mean = (a + b) * 0.5
        channel_dev = (a + b)[1:2] + ((a - b) * (a - b))[0:1] * (TOK * RING * 0.5)
        channel = lax.broadcasted_iota(jnp.int32, (CH, ROW), 0)
        group = lax.broadcasted_iota(jnp.int32, (CH, ROW), 1) * GROUP_CH
        member = ((channel >= group) & (channel < group + GROUP_CH)).astype(F32)

        def over_group(v):
            total = jnp.dot(jnp.broadcast_to(v, (8, CH)), member, precision=HIGHEST, preferred_element_type=F32)
            return lax.dot_general(total, member, NT, precision=HIGHEST, preferred_element_type=F32)[0:1]

        group_mean = over_group(both_mean[0:1]) * (1.0 / GROUP_CH)
        off = both_mean[0:1] - group_mean
        tokens = TOK * PATCHES
        variance = over_group(channel_dev + off * off * tokens) * (1.0 / (GROUP_CH * tokens))
        scale = lax.rsqrt(variance + EPSILON)

        load[D_GAIN].wait()
        load[D_SHIFT].wait()
        norm[0:1, :] = group_mean
        norm[1:2, :] = scale
        norm[2:3, :] = gain[...].reshape(1, CH)
        norm[3:4, :] = shift[...].reshape(1, CH)
        for r in (1, 2, 3):
            activate(r)

        load[D_TW].wait()
        load[D_STEP].wait()
        features_half = tw.shape[0] // 2
        j = lax.broadcasted_iota(jnp.int32, (16, features_half), 1).astype(F32)
        angle = timestep[0].astype(F32) * jnp.exp(j * (-math.log(10000.0) / features_half))
        cos, sin = jnp.cos(angle), jnp.sin(angle)
        cos = (cos / (1.0 + jnp.exp(-cos))).astype(BF16)
        sin = (sin / (1.0 + jnp.exp(-sin))).astype(BF16)
        time_shift = jnp.dot(cos, tw[0:features_half, :], preferred_element_type=F32) + jnp.dot(
            sin, tw[features_half:, :], preferred_element_type=F32
        )

        load[D_CONV].wait()
        conv_acc[...] = jnp.broadcast_to(time_shift[0:1], (TOK, CH))
        convolve(ROW, 0, TOK, 1)
        got("z0", "z1")
        go("pr0", "pl0")
        convolve(ROW, ROW, 2 * ROW, 0)
        convolve(2 * ROW, 0, 2 * ROW, 2)

    def outer_rows():
        @pl.when(me > 0)
        def _():
            down.wait_recv()

        @pl.when(me < PATCHES - 1)
        def _():
            up.wait_recv()

        activate(0)
        activate(4)
        convolve(0, 0, ROW, 0)
        convolve(4 * ROW, 2 * ROW, ROW, 2)
        res_ref[...] = conv_acc[...].astype(BF16)

    def one_step(step, carry):
        @pl.when(step == 1)
        def _():
            combine_ring()

            @pl.when(zh == 0)
            def _():
                pl.semaphore_wait(late_sem, 1)

            stat_p.start()

            @pl.when(zh == 0)
            def _():
                go("z0")

            go("z1", "z2", "z3")

            @pl.when(me == RING - 1)
            def _():
                pl.semaphore_wait(seam_sem, 1)

            got("r0", "l1")
            go("or", "ol")

            @pl.when((me < PATCHES - 1) & (me != RING - 1))
            def _():
                down.start()

            @pl.when((me > 0) & (me != RING))
            def _():
                up.start()

        @pl.when(step == 2)
        def _():
            got("r1", "l0")

        @pl.when(step == 3)
        def _():
            inner_rows()
            got("or", "ol")
            go("oz")

            @pl.when(me == RING - 1)
            def _():
                down.start()

            @pl.when(me == RING)
            def _():
                up.start()

        @pl.when(step == 4)
        def _():
            got("z2")
            go("pr2", "pl2")
            got("pr0", "pl0")
            go("po0", "po1")

        @pl.when(step == 5)
        def _():
            got("z3")
            go("pr3", "pl3")
            got("pr2")
            go("po2")

        @pl.when(step == 6)
        def _():
            got("pl2", "po0", "po1")

        @pl.when(step == 7)
        def _():
            @pl.when((me != RING - 1) & (me != RING))
            def _():
                outer_rows()

            got("pr3", "pl3", "po2", "oz")

        attend(step)
        return carry

    lax.fori_loop(0, PATCHES, one_step, 0)

    @pl.when((me == RING - 1) | (me == RING))
    def _():
        outer_rows()


    for p in range(PAIRS):
        total = acc[p]
        first = total[0:64, 0:TOK] / total[PAIR_CH : PAIR_CH + 1, 0:TOK]
        second = total[64:128, TOK:PAIR_Q] / total[PAIR_CH : PAIR_CH + 1, TOK:PAIR_Q]
        attn_ref[:, PAIR_CH * p : PAIR_CH * (p + 1)] = jnp.concatenate([first, second], axis=0).T.astype(BF16)

    for copy in (stat_r, stat_l, stat_o, stat_p):
        copy.wait_send()

    @pl.when(me < PATCHES - 1)
    def _():
        down.wait_send()

    @pl.when(me > 0)
    def _():
        up.wait_send()

    for name, copy in bulks.items():
        copy.wait_send()


def per_device(timestep, features, hidden, stale_hidden, gn_gain, gn_shift, conv_kernel, time_weight, wq, wk, wv):
    anywhere = pl.BlockSpec(memory_space=pl.ANY)
    vmem = pl.BlockSpec(memory_space=pltpu.VMEM)
    out = jax.ShapeDtypeStruct((TOK, CH), BF16)
    return pl.pallas_call(
        kernel,
        out_shape=(out, out),
        in_specs=[anywhere] * 11,
        out_specs=(vmem, vmem),
        scratch_shapes=[
            pltpu.VMEM((PATCHES, TOK, CH), BF16),
            pltpu.VMEM((TOK + 2 * ROW, CH), BF16),
            pltpu.VMEM((6, 8, CH), F32),
            pltpu.VMEM((CH, CH), BF16),
            pltpu.VMEM((CH, CH), BF16),
            pltpu.VMEM((CH, CH), BF16),
            pltpu.VMEM((CH, CH), BF16),
            pltpu.VMEM((320, CH), BF16),
            pltpu.VMEM((3, 3 * CH, CH), BF16),
            pltpu.VMEM((TOK + 2 * ROW, 3 * CH), BF16),
            pltpu.VMEM((PAIRS, PAIR_CH, PAIR_Q), BF16),
            pltpu.VMEM((TOK, CH), BF16),
            pltpu.VMEM((PAIRS, VROWS, TOK), BF16),
            pltpu.VMEM((2, TOK, PAIR_Q), F32),
            pltpu.VMEM((2, TOK, PAIR_Q), BF16),
            pltpu.VMEM((PAIRS, 1, PAIR_Q), F32),
            pltpu.VMEM((PAIRS, VROWS, PAIR_Q), F32),
            pltpu.VMEM((TOK, CH), F32),
            pltpu.VMEM((8, CH), F32),
            pltpu.VMEM((CH,), F32),
            pltpu.VMEM((CH,), F32),
            pltpu.SMEM((1,), jnp.int32),
            pltpu.SemaphoreType.DMA((N_SENDS,)),
            pltpu.SemaphoreType.DMA((6,)),
            pltpu.SemaphoreType.DMA((PATCHES, 8)),
            pltpu.SemaphoreType.DMA((10,)),
            pltpu.SemaphoreType.REGULAR,
            pltpu.SemaphoreType.REGULAR,
        ],
        compiler_params=pltpu.CompilerParams(
            collective_id=0, has_side_effects=True, vmem_limit_bytes=56 * 2**20
        ),
    )(
        timestep, features, hidden, stale_hidden, gn_gain, gn_shift,
        conv_kernel.reshape(3, 3 * CH, CH), time_weight, wq, wk, wv,
    )


def solution(mesh):
    tokens = P(("batch", "patch"), None)
    return jax.shard_map(
        per_device,
        mesh=mesh,
        in_specs=(P("batch"), tokens, tokens, tokens) + (P(),) * 7,
        out_specs=(tokens, tokens),
        check_vma=False,
    )
```

```python
import functools
import math

import jax
import jax.numpy as jnp
from jax import lax
from jax.experimental import pallas as pl
from jax.experimental.pallas import tpu as pltpu
from jax.sharding import PartitionSpec as P

F32, BF16 = jnp.float32, jnp.bfloat16
MESH = pl.DeviceIdType.MESH
NT = (((1,), (1,)), ((), ()))
HIGHEST = lax.Precision.HIGHEST
TOK, CH, ROW, HALF, QUARTER, EIGHTH = 384, 640, 128, 192, 96, 48
GROUPS, GROUP_CH, PATCHES, RING = 16, 40, 8, 4
PAIRS, PAIR_CH, PAIR_Q = 5, 128, 768
VROWS = 144
EPSILON = 1e-05
S_STAT_R, S_STAT_L, S_STAT_O, S_STAT_P, S_DOWN, S_UP = range(6)
S_BULK = 6
N_SENDS = S_BULK + 22
R_STAT_L, R_STAT_R, R_STAT_O, R_STAT_P, R_TOP, R_BOTTOM = range(6)
D_FEAT, D_HID, D_WQ, D_WK, D_WV, D_TW, D_CONV, D_GAIN, D_SHIFT, D_STEP = range(10)


def kernel(
    step_hbm, feat_hbm, hid_hbm, stale_hbm, gain_hbm, shift_hbm, conv_hbm, tw_hbm, wq_hbm, wk_hbm, wv_hbm,
    res_ref, attn_ref,
    keys, feats, stats, wq, wk, wv, wvt, tw, convw, act, qt, kbuf, vt, scores, probs,
    row_max, acc, conv_acc, norm, gain, shift, timestep, send_sem, recv_sem, bulk_sem, load_sem, late_sem, seam_sem,
):
    me = lax.axis_index("patch")
    y, zh = lax.rem(me, RING), lax.div(me, RING)
    right = {"patch": zh * RING + lax.rem(y + 1, RING)}
    left = {"patch": zh * RING + lax.rem(y + RING - 1, RING)}
    across = {"patch": zh * RING + lax.rem(y + 2, RING)}
    partner = {"patch": (1 - zh) * RING + y}

    barrier = pltpu.get_barrier_semaphore()
    for device in (right, left, across):
        pl.semaphore_signal(barrier, inc=1, device_id=device, device_id_type=MESH)

    @pl.when(zh == 0)
    def _():
        pl.semaphore_signal(barrier, inc=1, device_id=partner, device_id_type=MESH)

    @pl.when(me == RING - 1)
    def _():
        pl.semaphore_signal(barrier, inc=1, device_id={"patch": me + 1}, device_id_type=MESH)

    loads = [
        (D_FEAT, feat_hbm, feats.at[pl.ds(ROW, TOK)]),
        (D_HID, hid_hbm, keys.at[0]),
        (D_WQ, wq_hbm, wq),
        (D_WK, wk_hbm, wk),
        (D_WV, wv_hbm, wv),
        (D_TW, tw_hbm, tw),
        (D_CONV, conv_hbm, convw),
        (D_GAIN, gain_hbm, gain),
        (D_SHIFT, shift_hbm, shift),
        (D_STEP, step_hbm, timestep),
    ]
    load = {i: pltpu.make_async_copy(src, dst, load_sem.at[i]) for i, src, dst in loads}
    for i, _, _ in loads:
        if i != D_CONV:
            load[i].start()

    def remote(slot, src, dst, recv, device):
        return pltpu.make_async_remote_copy(
            src_ref=src, dst_ref=dst, send_sem=send_sem.at[slot], recv_sem=recv,
            device_id=device, device_id_type=MESH,
        )

    def rows(step, first, count):
        return keys.at[step, pl.ds(first, count)]

    def bulk(index, src, step, first, count, device):
        return remote(
            S_BULK + index, src, rows(step, first, count), bulk_sem.at[step, first // EIGHTH], device
        )

    def own(first, count):
        return stale_hbm.at[pl.ds(first, count)]

    moves = {
        "r0": (own(0, HALF), 1, 0, HALF, right),
        "l1": (own(HALF, HALF), 1, HALF, HALF, left),
        "r1": (own(HALF, HALF), 2, 0, HALF, right),
        "l0": (own(0, HALF), 2, HALF, HALF, left),
        "or": (rows(1, 0, HALF), 3, 0, HALF, right),
        "ol": (rows(1, HALF, HALF), 3, HALF, HALF, left),
        "z0": (own(0, QUARTER), 5, 0, QUARTER, partner),
        "z1": (own(QUARTER, QUARTER), 5, QUARTER, QUARTER, partner),
        "z2": (own(HALF, QUARTER), 5, HALF, QUARTER, partner),
        "z3": (own(HALF + QUARTER, QUARTER), 5, HALF + QUARTER, QUARTER, partner),
        "pr0": (rows(5, 0, HALF), 4, 0, HALF, right),
        "pl0": (rows(5, 0, HALF), 4, HALF, HALF, left),
        "pr2": (rows(5, HALF, QUARTER), 6, HALF, QUARTER, right),
        "pl2": (rows(5, HALF, QUARTER), 6, HALF + QUARTER, QUARTER, left),
        "pr3": (rows(5, HALF + QUARTER, QUARTER), 7, 0, QUARTER, right),
        "pl3": (rows(5, HALF + QUARTER, QUARTER), 7, QUARTER, QUARTER, left),
        "po0": (rows(4, 0, QUARTER), 6, 0, QUARTER, right),
        "po1": (rows(4, HALF + QUARTER, QUARTER), 6, QUARTER, QUARTER, left),
        "po2": (rows(6, HALF, QUARTER), 7, HALF, QUARTER, right),
        "oz": (rows(3, HALF + QUARTER, QUARTER), 7, HALF + QUARTER, QUARTER, partner),
    }
    bulks = {name: bulk(i, *move) for i, (name, move) in enumerate(moves.items())}

    def go(*names):
        for name in names:
            bulks[name].start()

    def got(*names):
        for name in names:
            bulks[name].wait_recv()

    def stat(slot, src, dst, recv, device):
        return remote(slot, stats.at[src], stats.at[dst], recv_sem.at[recv], device)

    stat_r = stat(S_STAT_R, 0, 1, R_STAT_L, right)
    stat_l = stat(S_STAT_L, 0, 2, R_STAT_R, left)
    stat_o = stat(S_STAT_O, 0, 3, R_STAT_O, across)
    stat_p = stat(S_STAT_P, 4, 5, R_STAT_P, partner)
    down = remote(S_DOWN, feat_hbm.at[pl.ds(TOK - ROW, ROW)], feats.at[pl.ds(0, ROW)], recv_sem.at[R_TOP], {"patch": me + 1})
    up = remote(S_UP, feat_hbm.at[pl.ds(0, ROW)], feats.at[pl.ds(ROW + TOK, ROW)], recv_sem.at[R_BOTTOM], {"patch": me - 1})

    @pl.when(me == 0)
    def _():
        feats[pl.ds(0, ROW), :] = jnp.zeros((ROW, CH), BF16)

    @pl.when(me == PATCHES - 1)
    def _():
        feats[pl.ds(ROW + TOK, ROW), :] = jnp.zeros((ROW, CH), BF16)

    def local_stats():
        load[D_FEAT].wait()
        x = feats[pl.ds(ROW, TOK), :].astype(F32)
        mean = jnp.sum(x, axis=0, keepdims=True) * (1.0 / TOK)
        stats[0, 0:1, :] = mean
        stats[0, 1:2, :] = jnp.sum((x - mean) * (x - mean), axis=0, keepdims=True)
        stats[0, 2:8, :] = jnp.zeros((6, CH), F32)

    def prepare():
        load[D_HID].wait()
        load[D_WQ].wait()
        query = jnp.dot(keys[0], wq[...], preferred_element_type=F32).astype(BF16).astype(F32) * 0.125
        zero = jnp.zeros((PAIR_CH // 2, TOK), BF16)
        for p in range(PAIRS):
            t = query[:, PAIR_CH * p : PAIR_CH * (p + 1)].T.astype(BF16)
            qt[p, 0:64, 0:TOK] = t[0:64]
            qt[p, 64:128, 0:TOK] = zero
            qt[p, 0:64, TOK:PAIR_Q] = zero
            qt[p, 64:128, TOK:PAIR_Q] = t[64:128]
            vt[p, PAIR_CH:VROWS, :] = jnp.ones((VROWS - PAIR_CH, TOK), BF16)
        load[D_WV].wait()
        wvt[...] = wv[...].astype(F32).T.astype(BF16)
        load[D_WK].wait()
        row_max[...] = jnp.full(row_max.shape, -1e30, F32)
        acc[...] = jnp.zeros(acc.shape, F32)

    def open_ring():
        @pl.when(zh == 0)
        def _():
            pl.semaphore_wait(barrier, 3)

        @pl.when((zh == 1) & (me != RING))
        def _():
            pl.semaphore_wait(barrier, 4)

        @pl.when(me == RING)
        def _():
            pl.semaphore_wait(barrier, 5)

        stat_r.start()
        stat_l.start()
        stat_o.start()
        go("r0", "l1")

        @pl.when(me == RING)
        def _():
            pl.semaphore_signal(seam_sem, inc=1, device_id={"patch": me - 1}, device_id_type=MESH)

        @pl.when(zh == 1)
        def _():
            pl.semaphore_signal(late_sem, inc=1, device_id=partner, device_id_type=MESH)
            go("z0")

        go("r1", "l0")


    early = (zh == 0) & (y < 2)
    local_stats()

    @pl.when(early)
    def _():
        prepare()

    open_ring()

    @pl.when(jnp.logical_not(early))
    def _():
        prepare()

    load[D_CONV].start()

    def attend(step):
        source = keys[step]
        kbuf[...] = jnp.dot(source, wk[...], preferred_element_type=F32).astype(BF16)
        value = lax.dot_general(wvt[...], source, NT, preferred_element_type=F32).astype(BF16)
        for p in range(PAIRS):
            vt[p, 0:PAIR_CH, :] = value[PAIR_CH * p : PAIR_CH * (p + 1), :]

        def score(p):
            scores[p % 2] = jnp.dot(
                kbuf[:, PAIR_CH * p : PAIR_CH * (p + 1)], qt[p], preferred_element_type=F32
            )

        def soften(p):
            s = scores[p % 2]
            old = row_max[p]
            new = jnp.maximum(old, jnp.max(s, axis=0, keepdims=True))
            probs[p % 2] = jnp.exp(s - new).astype(BF16)
            row_max[p] = new
            return jnp.exp(old - new)

        def weigh(p, factor):
            acc[p] = acc[p] * factor + jnp.dot(vt[p], probs[p % 2], preferred_element_type=F32)

        score(0)
        factor = None
        for p in range(PAIRS + 1):
            if p + 1 < PAIRS:
                score(p + 1)
            if p >= 1:
                weigh(p - 1, factor)
            if p < PAIRS:
                factor = soften(p)

    def combine_ring():
        stat_r.wait_recv()
        stat_l.wait_recv()
        stat_o.wait_recv()
        s4 = [stats[i] for i in range(4)]
        half_mean = (s4[0] + s4[1] + s4[2] + s4[3]) * 0.25
        half_dev = s4[0] + s4[1] + s4[2] + s4[3]
        spread = sum((s - half_mean) * (s - half_mean) for s in s4) * TOK
        stats[4, 0:1, :] = half_mean[0:1]
        stats[4, 1:2, :] = half_dev[1:2] + spread[0:1]
        stats[4, 2:8, :] = jnp.zeros((6, CH), F32)

    def activate(r):
        group_mean, scale, gain_row, shift_row = affine_rows()
        column = lax.broadcasted_iota(jnp.int32, (ROW, CH), 0)
        v = feats[pl.ds(r * ROW, ROW), :].astype(F32)
        v = (v - group_mean) * scale * gain_row + shift_row
        v = v / (1.0 + jnp.exp(-v))
        if r == 0:
            v = jnp.where(me == 0, 0.0, v)
        if r == 4:
            v = jnp.where(me == PATCHES - 1, 0.0, v)
        act[pl.ds(r * ROW, ROW), 0:CH] = jnp.where(column == 0, 0.0, pltpu.roll(v, 1, 0)).astype(BF16)
        act[pl.ds(r * ROW, ROW), CH : 2 * CH] = v.astype(BF16)
        act[pl.ds(r * ROW, ROW), 2 * CH : 3 * CH] = jnp.where(
            column == ROW - 1, 0.0, pltpu.roll(v, ROW - 1, 0)
        ).astype(BF16)

    def affine_rows():
        return norm[0:1, :], norm[1:2, :], norm[2:3, :], norm[3:4, :]

    def convolve(first_row, first_out, count, tap):
        conv_acc[pl.ds(first_out, count), :] += jnp.dot(
            act[pl.ds(first_row, count), :], convw[tap], preferred_element_type=F32
        )

    def inner_rows():
        stat_p.wait_recv()
        a, b = stats[4], stats[5]
        both_mean = (a + b) * 0.5
        channel_dev = (a + b)[1:2] + ((a - b) * (a - b))[0:1] * (TOK * RING * 0.5)
        channel = lax.broadcasted_iota(jnp.int32, (CH, ROW), 0)
        group = lax.broadcasted_iota(jnp.int32, (CH, ROW), 1) * GROUP_CH
        member = ((channel >= group) & (channel < group + GROUP_CH)).astype(F32)

        def over_group(v):
            total = jnp.dot(jnp.broadcast_to(v, (8, CH)), member, precision=HIGHEST, preferred_element_type=F32)
            return lax.dot_general(total, member, NT, precision=HIGHEST, preferred_element_type=F32)[0:1]

        group_mean = over_group(both_mean[0:1]) * (1.0 / GROUP_CH)
        off = both_mean[0:1] - group_mean
        tokens = TOK * PATCHES
        variance = over_group(channel_dev + off * off * tokens) * (1.0 / (GROUP_CH * tokens))
        scale = lax.rsqrt(variance + EPSILON)

        load[D_GAIN].wait()
        load[D_SHIFT].wait()
        norm[0:1, :] = group_mean
        norm[1:2, :] = scale
        norm[2:3, :] = gain[...].reshape(1, CH)
        norm[3:4, :] = shift[...].reshape(1, CH)
        for r in (1, 2, 3):
            activate(r)

        load[D_TW].wait()
        load[D_STEP].wait()
        features_half = tw.shape[0] // 2
        j = lax.broadcasted_iota(jnp.int32, (16, features_half), 1).astype(F32)
        angle = timestep[0].astype(F32) * jnp.exp(j * (-math.log(10000.0) / features_half))
        cos, sin = jnp.cos(angle), jnp.sin(angle)
        cos = (cos / (1.0 + jnp.exp(-cos))).astype(BF16)
        sin = (sin / (1.0 + jnp.exp(-sin))).astype(BF16)
        time_shift = jnp.dot(cos, tw[0:features_half, :], preferred_element_type=F32) + jnp.dot(
            sin, tw[features_half:, :], preferred_element_type=F32
        )

        load[D_CONV].wait()
        conv_acc[...] = jnp.broadcast_to(time_shift[0:1], (TOK, CH))
        convolve(ROW, 0, TOK, 1)
        got("z0", "z1")
        go("pr0", "pl0")
        convolve(ROW, ROW, 2 * ROW, 0)
        convolve(2 * ROW, 0, 2 * ROW, 2)

    def top_row():
        @pl.when(me > 0)
        def _():
            down.wait_recv()

        activate(0)
        convolve(0, 0, ROW, 0)

    def bottom_row():
        @pl.when(me < PATCHES - 1)
        def _():
            up.wait_recv()

        activate(4)
        convolve(4 * ROW, 2 * ROW, ROW, 2)

    def one_step(step, carry):
        @pl.when(step == 1)
        def _():
            combine_ring()

            @pl.when(zh == 0)
            def _():
                pl.semaphore_wait(late_sem, 1)

            stat_p.start()

            @pl.when(zh == 0)
            def _():
                go("z0")

            go("z1", "z2", "z3")

            @pl.when(me == RING - 1)
            def _():
                pl.semaphore_wait(seam_sem, 1)

            got("r0", "l1")
            go("or", "ol")

            @pl.when((me < PATCHES - 1) & (me != RING - 1))
            def _():
                down.start()

            @pl.when((me > 0) & (me != RING))
            def _():
                up.start()

        @pl.when(step == 2)
        def _():
            got("r1", "l0")

        @pl.when(step == 3)
        def _():
            inner_rows()
            got("or", "ol")
            go("oz")

            @pl.when(me == RING - 1)
            def _():
                down.start()

            @pl.when(me == RING)
            def _():
                up.start()

        @pl.when(step == 4)
        def _():
            got("z2")
            go("pr2", "pl2")
            got("pr0", "pl0")
            go("po0", "po1")

        @pl.when(step == 5)
        def _():
            got("z3")
            go("pr3", "pl3")
            got("pr2")
            go("po2")

        @pl.when(step == 6)
        def _():
            got("pl2", "po0", "po1")

        @pl.when(step == 7)
        def _():
            @pl.when(me != RING)
            def _():
                top_row()

            @pl.when(me != RING - 1)
            def _():
                bottom_row()

            got("pr3", "pl3", "po2", "oz")

        attend(step)
        return carry

    lax.fori_loop(0, PATCHES, one_step, 0)


    for p in range(PAIRS):
        total = acc[p]
        first = total[0:64, 0:TOK] / total[PAIR_CH : PAIR_CH + 1, 0:TOK]
        second = total[64:128, TOK:PAIR_Q] / total[PAIR_CH : PAIR_CH + 1, TOK:PAIR_Q]
        attn_ref[:, PAIR_CH * p : PAIR_CH * (p + 1)] = jnp.concatenate([first, second], axis=0).T.astype(BF16)

    @pl.when(me == RING)
    def _():
        top_row()

    @pl.when(me == RING - 1)
    def _():
        bottom_row()

    res_ref[...] = conv_acc[...].astype(BF16)

    for copy in (stat_r, stat_l, stat_o, stat_p):
        copy.wait_send()

    @pl.when(me < PATCHES - 1)
    def _():
        down.wait_send()

    @pl.when(me > 0)
    def _():
        up.wait_send()

    for name, copy in bulks.items():
        copy.wait_send()


def hand_on(res, attn, res_out, attn_out):
    res_out[...] = res[...]
    attn_out[...] = attn[...]


def per_device(timestep, features, hidden, stale_hidden, gn_gain, gn_shift, conv_kernel, time_weight, wq, wk, wv):
    anywhere = pl.BlockSpec(memory_space=pl.ANY)
    vmem = pl.BlockSpec(memory_space=pltpu.VMEM)
    out = jax.ShapeDtypeStruct((TOK, CH), BF16)
    made = pl.pallas_call(
        kernel,
        out_shape=(out, out),
        in_specs=[anywhere] * 11,
        out_specs=(vmem, vmem),
        scratch_shapes=[
            pltpu.VMEM((PATCHES, TOK, CH), BF16),
            pltpu.VMEM((TOK + 2 * ROW, CH), BF16),
            pltpu.VMEM((6, 8, CH), F32),
            pltpu.VMEM((CH, CH), BF16),
            pltpu.VMEM((CH, CH), BF16),
            pltpu.VMEM((CH, CH), BF16),
            pltpu.VMEM((CH, CH), BF16),
            pltpu.VMEM((320, CH), BF16),
            pltpu.VMEM((3, 3 * CH, CH), BF16),
            pltpu.VMEM((TOK + 2 * ROW, 3 * CH), BF16),
            pltpu.VMEM((PAIRS, PAIR_CH, PAIR_Q), BF16),
            pltpu.VMEM((TOK, CH), BF16),
            pltpu.VMEM((PAIRS, VROWS, TOK), BF16),
            pltpu.VMEM((2, TOK, PAIR_Q), F32),
            pltpu.VMEM((2, TOK, PAIR_Q), BF16),
            pltpu.VMEM((PAIRS, 1, PAIR_Q), F32),
            pltpu.VMEM((PAIRS, VROWS, PAIR_Q), F32),
            pltpu.VMEM((TOK, CH), F32),
            pltpu.VMEM((8, CH), F32),
            pltpu.VMEM((CH,), F32),
            pltpu.VMEM((CH,), F32),
            pltpu.SMEM((1,), jnp.int32),
            pltpu.SemaphoreType.DMA((N_SENDS,)),
            pltpu.SemaphoreType.DMA((6,)),
            pltpu.SemaphoreType.DMA((PATCHES, 8)),
            pltpu.SemaphoreType.DMA((10,)),
            pltpu.SemaphoreType.REGULAR,
            pltpu.SemaphoreType.REGULAR,
        ],
        compiler_params=pltpu.CompilerParams(
            collective_id=0, has_side_effects=True, vmem_limit_bytes=56 * 2**20
        ),
    )(
        timestep, features, hidden, stale_hidden, gn_gain, gn_shift,
        conv_kernel.reshape(3, 3 * CH, CH), time_weight, wq, wk, wv,
    )
    return pl.pallas_call(
        hand_on,
        out_shape=(out, out),
        in_specs=[vmem, vmem],
        out_specs=(vmem, vmem),
    )(*made)


def solution(mesh):
    tokens = P(("batch", "patch"), None)
    return jax.shard_map(
        per_device,
        mesh=mesh,
        in_specs=(P("batch"), tokens, tokens, tokens) + (P(),) * 7,
        out_specs=(tokens, tokens),
        check_vma=False,
    )
```

```python
import functools
import math

import jax
import jax.numpy as jnp
from jax import lax
from jax.experimental import pallas as pl
from jax.experimental.pallas import tpu as pltpu
from jax.sharding import PartitionSpec as P

F32, BF16 = jnp.float32, jnp.bfloat16
MESH = pl.DeviceIdType.MESH
NT = (((1,), (1,)), ((), ()))
HIGHEST = lax.Precision.HIGHEST
TOK, CH, ROW, HALF, QUARTER, EIGHTH = 384, 640, 128, 192, 96, 48
GROUPS, GROUP_CH, PATCHES, RING = 16, 40, 8, 4
PAIRS, PAIR_CH, PAIR_Q = 5, 128, 768
VROWS = 144
EPSILON = 1e-05
S_STAT_R, S_STAT_L, S_STAT_O, S_STAT_P, S_DOWN, S_UP, S_RELAY = range(7)
S_BULK = 7
N_SENDS = S_BULK + 22
R_STAT_L, R_STAT_R, R_STAT_O, R_STAT_P, R_TOP, R_BOTTOM = range(6)
D_FEAT, D_HID, D_WQ, D_WK, D_WV, D_TW, D_CONV, D_GAIN, D_SHIFT, D_STEP = range(10)


def kernel(
    step_hbm, feat_hbm, hid_hbm, stale_hbm, gain_hbm, shift_hbm, conv_hbm, tw_hbm, wq_hbm, wk_hbm, wv_hbm,
    res_ref, attn_ref,
    keys, feats, stats, wq, wk, wv, wvt, tw, convw, act, qt, kbuf, vt, scores, probs,
    row_max, acc, conv_acc, norm, gain, shift, timestep, send_sem, recv_sem, bulk_sem, load_sem, late_sem,
):
    me = lax.axis_index("patch")
    y, zh = lax.rem(me, RING), lax.div(me, RING)
    right = {"patch": zh * RING + lax.rem(y + 1, RING)}
    left = {"patch": zh * RING + lax.rem(y + RING - 1, RING)}
    across = {"patch": zh * RING + lax.rem(y + 2, RING)}
    partner = {"patch": (1 - zh) * RING + y}

    barrier = pltpu.get_barrier_semaphore()
    for device in (right, left, across):
        pl.semaphore_signal(barrier, inc=1, device_id=device, device_id_type=MESH)

    @pl.when(zh == 0)
    def _():
        pl.semaphore_signal(barrier, inc=1, device_id=partner, device_id_type=MESH)

    @pl.when(me == RING - 1)
    def _():
        pl.semaphore_signal(barrier, inc=1, device_id={"patch": me + 1}, device_id_type=MESH)

    loads = [
        (D_FEAT, feat_hbm, feats.at[pl.ds(ROW, TOK)]),
        (D_HID, hid_hbm, keys.at[0]),
        (D_WQ, wq_hbm, wq),
        (D_WK, wk_hbm, wk),
        (D_WV, wv_hbm, wv),
        (D_TW, tw_hbm, tw),
        (D_CONV, conv_hbm, convw),
        (D_GAIN, gain_hbm, gain),
        (D_SHIFT, shift_hbm, shift),
        (D_STEP, step_hbm, timestep),
    ]
    load = {i: pltpu.make_async_copy(src, dst, load_sem.at[i]) for i, src, dst in loads}
    for i, _, _ in loads:
        if i != D_CONV:
            load[i].start()

    def remote(slot, src, dst, recv, device):
        return pltpu.make_async_remote_copy(
            src_ref=src, dst_ref=dst, send_sem=send_sem.at[slot], recv_sem=recv,
            device_id=device, device_id_type=MESH,
        )

    def rows(step, first, count):
        return keys.at[step, pl.ds(first, count)]

    def bulk(index, src, step, first, count, device):
        return remote(
            S_BULK + index, src, rows(step, first, count), bulk_sem.at[step, first // EIGHTH], device
        )

    def own(first, count):
        return stale_hbm.at[pl.ds(first, count)]

    moves = {
        "r0": (own(0, HALF), 1, 0, HALF, right),
        "l1": (own(HALF, HALF), 1, HALF, HALF, left),
        "r1": (own(HALF, HALF), 2, 0, HALF, right),
        "l0": (own(0, HALF), 2, HALF, HALF, left),
        "or": (rows(1, 0, HALF), 3, 0, HALF, right),
        "ol": (rows(1, HALF, HALF), 3, HALF, HALF, left),
        "z0": (own(0, QUARTER), 5, 0, QUARTER, partner),
        "z1": (own(QUARTER, QUARTER), 5, QUARTER, QUARTER, partner),
        "z2": (own(HALF, QUARTER), 5, HALF, QUARTER, partner),
        "z3": (own(HALF + QUARTER, QUARTER), 5, HALF + QUARTER, QUARTER, partner),
        "pr0": (rows(5, 0, HALF), 4, 0, HALF, right),
        "pl0": (rows(5, 0, HALF), 4, HALF, HALF, left),
        "pr2": (rows(5, HALF, QUARTER), 6, HALF, QUARTER, right),
        "pl2": (rows(5, HALF, QUARTER), 6, HALF + QUARTER, QUARTER, left),
        "pr3": (rows(5, HALF + QUARTER, QUARTER), 7, 0, QUARTER, right),
        "pl3": (rows(5, HALF + QUARTER, QUARTER), 7, QUARTER, QUARTER, left),
        "po0": (rows(4, 0, QUARTER), 6, 0, QUARTER, right),
        "po1": (rows(4, HALF + QUARTER, QUARTER), 6, QUARTER, QUARTER, left),
        "po2": (rows(6, HALF, QUARTER), 7, HALF, QUARTER, right),
        "oz": (rows(3, HALF + QUARTER, QUARTER), 7, HALF + QUARTER, QUARTER, partner),
    }
    bulks = {name: bulk(i, *move) for i, (name, move) in enumerate(moves.items())}

    def go(*names):
        for name in names:
            bulks[name].start()

    def got(*names):
        for name in names:
            bulks[name].wait_recv()

    def stat(slot, src, dst, recv, device):
        return remote(slot, stats.at[src], stats.at[dst], recv_sem.at[recv], device)

    stat_r = stat(S_STAT_R, 0, 1, R_STAT_L, right)
    stat_l = stat(S_STAT_L, 0, 2, R_STAT_R, left)
    stat_o = stat(S_STAT_O, 0, 3, R_STAT_O, across)
    stat_p = stat(S_STAT_P, 4, 5, R_STAT_P, partner)
    down = remote(S_DOWN, feat_hbm.at[pl.ds(TOK - ROW, ROW)], feats.at[pl.ds(0, ROW)], recv_sem.at[R_TOP], right)
    relay = remote(S_RELAY, feats.at[pl.ds(0, ROW)], feats.at[pl.ds(0, ROW)], recv_sem.at[R_TOP], partner)
    up = remote(S_UP, feat_hbm.at[pl.ds(0, ROW)], feats.at[pl.ds(ROW + TOK, ROW)], recv_sem.at[R_BOTTOM], {"patch": me - 1})

    @pl.when(me == PATCHES - 1)
    def _():
        feats[pl.ds(ROW + TOK, ROW), :] = jnp.zeros((ROW, CH), BF16)

    def local_stats():
        load[D_FEAT].wait()
        x = feats[pl.ds(ROW, TOK), :].astype(F32)
        mean = jnp.sum(x, axis=0, keepdims=True) * (1.0 / TOK)
        stats[0, 0:1, :] = mean
        stats[0, 1:2, :] = jnp.sum((x - mean) * (x - mean), axis=0, keepdims=True)
        stats[0, 2:8, :] = jnp.zeros((6, CH), F32)

    def prepare():
        load[D_HID].wait()
        load[D_WQ].wait()
        query = jnp.dot(keys[0], wq[...], preferred_element_type=F32).astype(BF16).astype(F32) * 0.125
        zero = jnp.zeros((PAIR_CH // 2, TOK), BF16)
        for p in range(PAIRS):
            t = query[:, PAIR_CH * p : PAIR_CH * (p + 1)].T.astype(BF16)
            qt[p, 0:64, 0:TOK] = t[0:64]
            qt[p, 64:128, 0:TOK] = zero
            qt[p, 0:64, TOK:PAIR_Q] = zero
            qt[p, 64:128, TOK:PAIR_Q] = t[64:128]
            vt[p, PAIR_CH:VROWS, :] = jnp.ones((VROWS - PAIR_CH, TOK), BF16)
        load[D_WV].wait()
        wvt[...] = wv[...].astype(F32).T.astype(BF16)
        load[D_WK].wait()
        row_max[...] = jnp.full(row_max.shape, -1e30, F32)
        acc[...] = jnp.zeros(acc.shape, F32)

    def open_ring():
        @pl.when(zh == 0)
        def _():
            pl.semaphore_wait(barrier, 3)

        @pl.when((zh == 1) & (me != RING))
        def _():
            pl.semaphore_wait(barrier, 4)

        @pl.when(me == RING)
        def _():
            pl.semaphore_wait(barrier, 5)

        stat_r.start()
        stat_l.start()
        stat_o.start()
        go("r0", "l1")

        @pl.when(zh == 1)
        def _():
            pl.semaphore_signal(late_sem, inc=1, device_id=partner, device_id_type=MESH)
            go("z0")

        go("r1", "l0")


    early = (zh == 0) & (y < 2)
    local_stats()

    @pl.when(early)
    def _():
        prepare()

    open_ring()

    @pl.when(jnp.logical_not(early))
    def _():
        prepare()

    load[D_CONV].start()

    def attend(step):
        source = keys[step]
        kbuf[...] = jnp.dot(source, wk[...], preferred_element_type=F32).astype(BF16)
        value = lax.dot_general(wvt[...], source, NT, preferred_element_type=F32).astype(BF16)
        for p in range(PAIRS):
            vt[p, 0:PAIR_CH, :] = value[PAIR_CH * p : PAIR_CH * (p + 1), :]

        def score(p):
            scores[p % 2] = jnp.dot(
                kbuf[:, PAIR_CH * p : PAIR_CH * (p + 1)], qt[p], preferred_element_type=F32
            )

        def soften(p):
            s = scores[p % 2]
            old = row_max[p]
            new = jnp.maximum(old, jnp.max(s, axis=0, keepdims=True))
            probs[p % 2] = jnp.exp(s - new).astype(BF16)
            row_max[p] = new
            return jnp.exp(old - new)

        def weigh(p, factor):
            acc[p] = acc[p] * factor + jnp.dot(vt[p], probs[p % 2], preferred_element_type=F32)

        score(0)
        factor = None
        for p in range(PAIRS + 1):
            if p + 1 < PAIRS:
                score(p + 1)
            if p >= 1:
                weigh(p - 1, factor)
            if p < PAIRS:
                factor = soften(p)

    def combine_ring():
        stat_r.wait_recv()
        stat_l.wait_recv()
        stat_o.wait_recv()
        s4 = [stats[i] for i in range(4)]
        half_mean = (s4[0] + s4[1] + s4[2] + s4[3]) * 0.25
        half_dev = s4[0] + s4[1] + s4[2] + s4[3]
        spread = sum((s - half_mean) * (s - half_mean) for s in s4) * TOK
        stats[4, 0:1, :] = half_mean[0:1]
        stats[4, 1:2, :] = half_dev[1:2] + spread[0:1]
        stats[4, 2:8, :] = jnp.zeros((6, CH), F32)

    def activate(r):
        group_mean, scale, gain_row, shift_row = affine_rows()
        column = lax.broadcasted_iota(jnp.int32, (ROW, CH), 0)
        v = feats[pl.ds(r * ROW, ROW), :].astype(F32)
        v = (v - group_mean) * scale * gain_row + shift_row
        v = v / (1.0 + jnp.exp(-v))
        if r == 0:
            v = jnp.where(me == 0, 0.0, v)
        if r == 4:
            v = jnp.where(me == PATCHES - 1, 0.0, v)
        act[pl.ds(r * ROW, ROW), 0:CH] = jnp.where(column == 0, 0.0, pltpu.roll(v, 1, 0)).astype(BF16)
        act[pl.ds(r * ROW, ROW), CH : 2 * CH] = v.astype(BF16)
        act[pl.ds(r * ROW, ROW), 2 * CH : 3 * CH] = jnp.where(
            column == ROW - 1, 0.0, pltpu.roll(v, ROW - 1, 0)
        ).astype(BF16)

    def affine_rows():
        return norm[0:1, :], norm[1:2, :], norm[2:3, :], norm[3:4, :]

    def convolve(first_row, first_out, count, tap):
        conv_acc[pl.ds(first_out, count), :] += jnp.dot(
            act[pl.ds(first_row, count), :], convw[tap], preferred_element_type=F32
        )

    def inner_rows():
        stat_p.wait_recv()
        a, b = stats[4], stats[5]
        both_mean = (a + b) * 0.5
        channel_dev = (a + b)[1:2] + ((a - b) * (a - b))[0:1] * (TOK * RING * 0.5)
        channel = lax.broadcasted_iota(jnp.int32, (CH, ROW), 0)
        group = lax.broadcasted_iota(jnp.int32, (CH, ROW), 1) * GROUP_CH
        member = ((channel >= group) & (channel < group + GROUP_CH)).astype(F32)

        def over_group(v):
            total = jnp.dot(jnp.broadcast_to(v, (8, CH)), member, precision=HIGHEST, preferred_element_type=F32)
            return lax.dot_general(total, member, NT, precision=HIGHEST, preferred_element_type=F32)[0:1]

        group_mean = over_group(both_mean[0:1]) * (1.0 / GROUP_CH)
        off = both_mean[0:1] - group_mean
        tokens = TOK * PATCHES
        variance = over_group(channel_dev + off * off * tokens) * (1.0 / (GROUP_CH * tokens))
        scale = lax.rsqrt(variance + EPSILON)

        load[D_GAIN].wait()
        load[D_SHIFT].wait()
        norm[0:1, :] = group_mean
        norm[1:2, :] = scale
        norm[2:3, :] = gain[...].reshape(1, CH)
        norm[3:4, :] = shift[...].reshape(1, CH)
        for r in (1, 2, 3):
            activate(r)

        load[D_TW].wait()
        load[D_STEP].wait()
        features_half = tw.shape[0] // 2
        j = lax.broadcasted_iota(jnp.int32, (16, features_half), 1).astype(F32)
        angle = timestep[0].astype(F32) * jnp.exp(j * (-math.log(10000.0) / features_half))
        cos, sin = jnp.cos(angle), jnp.sin(angle)
        cos = (cos / (1.0 + jnp.exp(-cos))).astype(BF16)
        sin = (sin / (1.0 + jnp.exp(-sin))).astype(BF16)
        time_shift = jnp.dot(cos, tw[0:features_half, :], preferred_element_type=F32) + jnp.dot(
            sin, tw[features_half:, :], preferred_element_type=F32
        )

        load[D_CONV].wait()
        conv_acc[...] = jnp.broadcast_to(time_shift[0:1], (TOK, CH))
        convolve(ROW, 0, TOK, 1)
        got("z0", "z1")
        go("pr0", "pl0")
        convolve(ROW, ROW, 2 * ROW, 0)
        convolve(2 * ROW, 0, 2 * ROW, 2)

    def top_row():
        @pl.when(me > 0)
        def _():
            down.wait_recv()

        activate(0)
        convolve(0, 0, ROW, 0)

    def bottom_row():
        @pl.when(me < PATCHES - 1)
        def _():
            up.wait_recv()

        activate(4)
        convolve(4 * ROW, 2 * ROW, ROW, 2)

    def one_step(step, carry):
        @pl.when(step == 1)
        def _():
            combine_ring()

            @pl.when(zh == 0)
            def _():
                pl.semaphore_wait(late_sem, 1)

            stat_p.start()

            @pl.when(zh == 0)
            def _():
                go("z0")

            go("z1", "z2", "z3")

            got("r0", "l1")
            go("or", "ol")

            @pl.when(me < PATCHES - 1)
            def _():
                down.start()

            @pl.when((me > 0) & (me != RING))
            def _():
                up.start()

        @pl.when(step == 2)
        def _():
            got("r1", "l0")

        @pl.when(step == 3)
        def _():
            inner_rows()
            got("or", "ol")

            @pl.when(me == 0)
            def _():
                down.wait_recv()
                relay.start()

            go("oz")


            @pl.when(me == RING)
            def _():
                up.start()

        @pl.when(step == 4)
        def _():
            got("z2")
            go("pr2", "pl2")
            got("pr0", "pl0")
            go("po0", "po1")

        @pl.when(step == 5)
        def _():
            got("z3")
            go("pr3", "pl3")
            got("pr2")
            go("po2")

        @pl.when(step == 6)
        def _():
            got("pl2", "po0", "po1")

        @pl.when(step == 7)
        def _():
            @pl.when(me != RING)
            def _():
                top_row()

            @pl.when(me != RING - 1)
            def _():
                bottom_row()

            got("pr3", "pl3", "po2", "oz")

        attend(step)
        return carry

    lax.fori_loop(0, PATCHES, one_step, 0)


    for p in range(PAIRS):
        total = acc[p]
        first = total[0:64, 0:TOK] / total[PAIR_CH : PAIR_CH + 1, 0:TOK]
        second = total[64:128, TOK:PAIR_Q] / total[PAIR_CH : PAIR_CH + 1, TOK:PAIR_Q]
        attn_ref[:, PAIR_CH * p : PAIR_CH * (p + 1)] = jnp.concatenate([first, second], axis=0).T.astype(BF16)

    @pl.when(me == RING)
    def _():
        top_row()

    @pl.when(me == RING - 1)
    def _():
        bottom_row()

    res_ref[...] = conv_acc[...].astype(BF16)

    for copy in (stat_r, stat_l, stat_o, stat_p):
        copy.wait_send()

    @pl.when(me == 0)
    def _():
        relay.wait_send()

    @pl.when(me < PATCHES - 1)
    def _():
        down.wait_send()

    @pl.when(me > 0)
    def _():
        up.wait_send()

    for name, copy in bulks.items():
        copy.wait_send()


def hand_on(res, attn, res_out, attn_out):
    res_out[...] = res[...]
    attn_out[...] = attn[...]


def per_device(timestep, features, hidden, stale_hidden, gn_gain, gn_shift, conv_kernel, time_weight, wq, wk, wv):
    anywhere = pl.BlockSpec(memory_space=pl.ANY)
    vmem = pl.BlockSpec(memory_space=pltpu.VMEM)
    out = jax.ShapeDtypeStruct((TOK, CH), BF16)
    made = pl.pallas_call(
        kernel,
        out_shape=(out, out),
        in_specs=[anywhere] * 11,
        out_specs=(vmem, vmem),
        scratch_shapes=[
            pltpu.VMEM((PATCHES, TOK, CH), BF16),
            pltpu.VMEM((TOK + 2 * ROW, CH), BF16),
            pltpu.VMEM((6, 8, CH), F32),
            pltpu.VMEM((CH, CH), BF16),
            pltpu.VMEM((CH, CH), BF16),
            pltpu.VMEM((CH, CH), BF16),
            pltpu.VMEM((CH, CH), BF16),
            pltpu.VMEM((320, CH), BF16),
            pltpu.VMEM((3, 3 * CH, CH), BF16),
            pltpu.VMEM((TOK + 2 * ROW, 3 * CH), BF16),
            pltpu.VMEM((PAIRS, PAIR_CH, PAIR_Q), BF16),
            pltpu.VMEM((TOK, CH), BF16),
            pltpu.VMEM((PAIRS, VROWS, TOK), BF16),
            pltpu.VMEM((2, TOK, PAIR_Q), F32),
            pltpu.VMEM((2, TOK, PAIR_Q), BF16),
            pltpu.VMEM((PAIRS, 1, PAIR_Q), F32),
            pltpu.VMEM((PAIRS, VROWS, PAIR_Q), F32),
            pltpu.VMEM((TOK, CH), F32),
            pltpu.VMEM((8, CH), F32),
            pltpu.VMEM((CH,), F32),
            pltpu.VMEM((CH,), F32),
            pltpu.SMEM((1,), jnp.int32),
            pltpu.SemaphoreType.DMA((N_SENDS,)),
            pltpu.SemaphoreType.DMA((6,)),
            pltpu.SemaphoreType.DMA((PATCHES, 8)),
            pltpu.SemaphoreType.DMA((10,)),
            pltpu.SemaphoreType.REGULAR,
        ],
        compiler_params=pltpu.CompilerParams(
            collective_id=0, has_side_effects=True, vmem_limit_bytes=56 * 2**20
        ),
    )(
        timestep, features, hidden, stale_hidden, gn_gain, gn_shift,
        conv_kernel.reshape(3, 3 * CH, CH), time_weight, wq, wk, wv,
    )
    return pl.pallas_call(
        hand_on,
        out_shape=(out, out),
        in_specs=[vmem, vmem],
        out_specs=(vmem, vmem),
    )(*made)


def solution(mesh):
    tokens = P(("batch", "patch"), None)
    return jax.shard_map(
        per_device,
        mesh=mesh,
        in_specs=(P("batch"), tokens, tokens, tokens) + (P(),) * 7,
        out_specs=(tokens, tokens),
        check_vma=False,
    )
```

```python
import functools
import math

import jax
import jax.numpy as jnp
from jax import lax
from jax.experimental import pallas as pl
from jax.experimental.pallas import tpu as pltpu
from jax.sharding import PartitionSpec as P

F32, BF16 = jnp.float32, jnp.bfloat16
MESH = pl.DeviceIdType.MESH
NT = (((1,), (1,)), ((), ()))
HIGHEST = lax.Precision.HIGHEST
TOK, CH, ROW, HALF, QUARTER, EIGHTH = 384, 640, 128, 192, 96, 48
GROUPS, GROUP_CH, PATCHES, RING = 16, 40, 8, 4
PAIRS, PAIR_CH, PAIR_Q = 5, 128, 768
VROWS = 144
EPSILON = 1e-05
S_STAT_R, S_STAT_L, S_STAT_O, S_STAT_P, S_DOWN, S_UP, S_RELAY, S_RELAY_UP = range(8)
S_BULK = 8
N_SENDS = S_BULK + 22
R_STAT_L, R_STAT_R, R_STAT_O, R_STAT_P, R_TOP, R_BOTTOM = range(6)
D_FEAT, D_HID, D_WQ, D_WK, D_WV, D_TW, D_CONV, D_GAIN, D_SHIFT, D_STEP = range(10)


def kernel(
    step_hbm, feat_hbm, hid_hbm, stale_hbm, gain_hbm, shift_hbm, conv_hbm, tw_hbm, wq_hbm, wk_hbm, wv_hbm,
    res_ref, attn_ref,
    keys, feats, stats, wq, wk, wv, wvt, tw, convw, act, qt, kbuf, vt, scores, probs,
    row_max, acc, conv_acc, norm, gain, shift, timestep, send_sem, recv_sem, bulk_sem, load_sem, late_sem,
):
    me = lax.axis_index("patch")
    y, zh = lax.rem(me, RING), lax.div(me, RING)
    right = {"patch": zh * RING + lax.rem(y + 1, RING)}
    left = {"patch": zh * RING + lax.rem(y + RING - 1, RING)}
    across = {"patch": zh * RING + lax.rem(y + 2, RING)}
    partner = {"patch": (1 - zh) * RING + y}

    barrier = pltpu.get_barrier_semaphore()
    for device in (right, left, across):
        pl.semaphore_signal(barrier, inc=1, device_id=device, device_id_type=MESH)

    @pl.when(zh == 0)
    def _():
        pl.semaphore_signal(barrier, inc=1, device_id=partner, device_id_type=MESH)

    loads = [
        (D_FEAT, feat_hbm, feats.at[pl.ds(ROW, TOK)]),
        (D_HID, hid_hbm, keys.at[0]),
        (D_WQ, wq_hbm, wq),
        (D_WK, wk_hbm, wk),
        (D_WV, wv_hbm, wv),
        (D_TW, tw_hbm, tw),
        (D_CONV, conv_hbm, convw),
        (D_GAIN, gain_hbm, gain),
        (D_SHIFT, shift_hbm, shift),
        (D_STEP, step_hbm, timestep),
    ]
    load = {i: pltpu.make_async_copy(src, dst, load_sem.at[i]) for i, src, dst in loads}
    for i, _, _ in loads:
        if i != D_CONV:
            load[i].start()

    def remote(slot, src, dst, recv, device):
        return pltpu.make_async_remote_copy(
            src_ref=src, dst_ref=dst, send_sem=send_sem.at[slot], recv_sem=recv,
            device_id=device, device_id_type=MESH,
        )

    def rows(step, first, count):
        return keys.at[step, pl.ds(first, count)]

    def bulk(index, src, step, first, count, device):
        return remote(
            S_BULK + index, src, rows(step, first, count), bulk_sem.at[step, first // EIGHTH], device
        )

    def own(first, count):
        return stale_hbm.at[pl.ds(first, count)]

    moves = {
        "r0": (own(0, HALF), 1, 0, HALF, right),
        "l1": (own(HALF, HALF), 1, HALF, HALF, left),
        "r1": (own(HALF, HALF), 2, 0, HALF, right),
        "l0": (own(0, HALF), 2, HALF, HALF, left),
        "or": (rows(1, 0, HALF), 3, 0, HALF, right),
        "ol": (rows(1, HALF, HALF), 3, HALF, HALF, left),
        "z0": (own(0, QUARTER), 5, 0, QUARTER, partner),
        "z1": (own(QUARTER, QUARTER), 5, QUARTER, QUARTER, partner),
        "z2": (own(HALF, QUARTER), 5, HALF, QUARTER, partner),
        "z3": (own(HALF + QUARTER, QUARTER), 5, HALF + QUARTER, QUARTER, partner),
        "pr0": (rows(5, 0, HALF), 4, 0, HALF, right),
        "pl0": (rows(5, 0, HALF), 4, HALF, HALF, left),
        "pr2": (rows(5, HALF, QUARTER), 6, HALF, QUARTER, right),
        "pl2": (rows(5, HALF, QUARTER), 6, HALF + QUARTER, QUARTER, left),
        "pr3": (rows(5, HALF + QUARTER, QUARTER), 7, 0, QUARTER, right),
        "pl3": (rows(5, HALF + QUARTER, QUARTER), 7, QUARTER, QUARTER, left),
        "po0": (rows(4, 0, QUARTER), 6, 0, QUARTER, right),
        "po1": (rows(4, HALF + QUARTER, QUARTER), 6, QUARTER, QUARTER, left),
        "po2": (rows(6, HALF, QUARTER), 7, HALF, QUARTER, right),
        "oz": (rows(3, HALF + QUARTER, QUARTER), 7, HALF + QUARTER, QUARTER, partner),
    }
    bulks = {name: bulk(i, *move) for i, (name, move) in enumerate(moves.items())}

    def go(*names):
        for name in names:
            bulks[name].start()

    def got(*names):
        for name in names:
            bulks[name].wait_recv()

    def stat(slot, src, dst, recv, device):
        return remote(slot, stats.at[src], stats.at[dst], recv_sem.at[recv], device)

    stat_r = stat(S_STAT_R, 0, 1, R_STAT_L, right)
    stat_l = stat(S_STAT_L, 0, 2, R_STAT_R, left)
    stat_o = stat(S_STAT_O, 0, 3, R_STAT_O, across)
    stat_p = stat(S_STAT_P, 4, 5, R_STAT_P, partner)
    down = remote(S_DOWN, feat_hbm.at[pl.ds(TOK - ROW, ROW)], feats.at[pl.ds(0, ROW)], recv_sem.at[R_TOP], right)
    relay_up = remote(S_RELAY_UP, feats.at[pl.ds(ROW + TOK, ROW)], feats.at[pl.ds(ROW + TOK, ROW)], recv_sem.at[R_BOTTOM], partner)
    relay = remote(S_RELAY, feats.at[pl.ds(0, ROW)], feats.at[pl.ds(0, ROW)], recv_sem.at[R_TOP], partner)
    up = remote(S_UP, feat_hbm.at[pl.ds(0, ROW)], feats.at[pl.ds(ROW + TOK, ROW)], recv_sem.at[R_BOTTOM], left)

    def local_stats():
        load[D_FEAT].wait()
        x = feats[pl.ds(ROW, TOK), :].astype(F32)
        mean = jnp.sum(x, axis=0, keepdims=True) * (1.0 / TOK)
        stats[0, 0:1, :] = mean
        stats[0, 1:2, :] = jnp.sum((x - mean) * (x - mean), axis=0, keepdims=True)
        stats[0, 2:8, :] = jnp.zeros((6, CH), F32)

    def prepare():
        load[D_HID].wait()
        load[D_WQ].wait()
        query = jnp.dot(keys[0], wq[...], preferred_element_type=F32).astype(BF16).astype(F32) * 0.125
        zero = jnp.zeros((PAIR_CH // 2, TOK), BF16)
        for p in range(PAIRS):
            t = query[:, PAIR_CH * p : PAIR_CH * (p + 1)].T.astype(BF16)
            qt[p, 0:64, 0:TOK] = t[0:64]
            qt[p, 64:128, 0:TOK] = zero
            qt[p, 0:64, TOK:PAIR_Q] = zero
            qt[p, 64:128, TOK:PAIR_Q] = t[64:128]
            vt[p, PAIR_CH:VROWS, :] = jnp.ones((VROWS - PAIR_CH, TOK), BF16)
        load[D_WV].wait()
        wvt[...] = wv[...].astype(F32).T.astype(BF16)
        load[D_WK].wait()
        row_max[...] = jnp.full(row_max.shape, -1e30, F32)
        acc[...] = jnp.zeros(acc.shape, F32)

    def open_ring():
        @pl.when(zh == 0)
        def _():
            pl.semaphore_wait(barrier, 3)

        @pl.when(zh == 1)
        def _():
            pl.semaphore_wait(barrier, 4)

        stat_r.start()
        stat_l.start()
        stat_o.start()
        go("r0", "l1")

        @pl.when(zh == 1)
        def _():
            pl.semaphore_signal(late_sem, inc=1, device_id=partner, device_id_type=MESH)
            go("z0")

        go("r1", "l0")


    early = (zh == 0) & (y < 2)
    local_stats()

    @pl.when(early)
    def _():
        prepare()

    open_ring()

    @pl.when(jnp.logical_not(early))
    def _():
        prepare()

    load[D_CONV].start()

    def attend(step):
        source = keys[step]
        kbuf[...] = jnp.dot(source, wk[...], preferred_element_type=F32).astype(BF16)
        value = lax.dot_general(wvt[...], source, NT, preferred_element_type=F32).astype(BF16)
        for p in range(PAIRS):
            vt[p, 0:PAIR_CH, :] = value[PAIR_CH * p : PAIR_CH * (p + 1), :]

        def score(p):
            scores[p % 2] = jnp.dot(
                kbuf[:, PAIR_CH * p : PAIR_CH * (p + 1)], qt[p], preferred_element_type=F32
            )

        def soften(p):
            s = scores[p % 2]
            old = row_max[p]
            new = jnp.maximum(old, jnp.max(s, axis=0, keepdims=True))
            probs[p % 2] = jnp.exp(s - new).astype(BF16)
            row_max[p] = new
            return jnp.exp(old - new)

        def weigh(p, factor):
            acc[p] = acc[p] * factor + jnp.dot(vt[p], probs[p % 2], preferred_element_type=F32)

        score(0)
        factor = None
        for p in range(PAIRS + 1):
            if p + 1 < PAIRS:
                score(p + 1)
            if p >= 1:
                weigh(p - 1, factor)
            if p < PAIRS:
                factor = soften(p)

    def combine_ring():
        stat_r.wait_recv()
        stat_l.wait_recv()
        stat_o.wait_recv()
        s4 = [stats[i] for i in range(4)]
        half_mean = (s4[0] + s4[1] + s4[2] + s4[3]) * 0.25
        half_dev = s4[0] + s4[1] + s4[2] + s4[3]
        spread = sum((s - half_mean) * (s - half_mean) for s in s4) * TOK
        stats[4, 0:1, :] = half_mean[0:1]
        stats[4, 1:2, :] = half_dev[1:2] + spread[0:1]
        stats[4, 2:8, :] = jnp.zeros((6, CH), F32)

    def activate(r):
        group_mean, scale, gain_row, shift_row = affine_rows()
        column = lax.broadcasted_iota(jnp.int32, (ROW, CH), 0)
        v = feats[pl.ds(r * ROW, ROW), :].astype(F32)
        v = (v - group_mean) * scale * gain_row + shift_row
        v = v / (1.0 + jnp.exp(-v))
        if r == 0:
            v = jnp.where(me == 0, 0.0, v)
        if r == 4:
            v = jnp.where(me == PATCHES - 1, 0.0, v)
        act[pl.ds(r * ROW, ROW), 0:CH] = jnp.where(column == 0, 0.0, pltpu.roll(v, 1, 0)).astype(BF16)
        act[pl.ds(r * ROW, ROW), CH : 2 * CH] = v.astype(BF16)
        act[pl.ds(r * ROW, ROW), 2 * CH : 3 * CH] = jnp.where(
            column == ROW - 1, 0.0, pltpu.roll(v, ROW - 1, 0)
        ).astype(BF16)

    def affine_rows():
        return norm[0:1, :], norm[1:2, :], norm[2:3, :], norm[3:4, :]

    def convolve(first_row, first_out, count, tap):
        conv_acc[pl.ds(first_out, count), :] += jnp.dot(
            act[pl.ds(first_row, count), :], convw[tap], preferred_element_type=F32
        )

    def inner_rows():
        stat_p.wait_recv()
        a, b = stats[4], stats[5]
        both_mean = (a + b) * 0.5
        channel_dev = (a + b)[1:2] + ((a - b) * (a - b))[0:1] * (TOK * RING * 0.5)
        channel = lax.broadcasted_iota(jnp.int32, (CH, ROW), 0)
        group = lax.broadcasted_iota(jnp.int32, (CH, ROW), 1) * GROUP_CH
        member = ((channel >= group) & (channel < group + GROUP_CH)).astype(F32)

        def over_group(v):
            total = jnp.dot(jnp.broadcast_to(v, (8, CH)), member, precision=HIGHEST, preferred_element_type=F32)
            return lax.dot_general(total, member, NT, precision=HIGHEST, preferred_element_type=F32)[0:1]

        group_mean = over_group(both_mean[0:1]) * (1.0 / GROUP_CH)
        off = both_mean[0:1] - group_mean
        tokens = TOK * PATCHES
        variance = over_group(channel_dev + off * off * tokens) * (1.0 / (GROUP_CH * tokens))
        scale = lax.rsqrt(variance + EPSILON)

        load[D_GAIN].wait()
        load[D_SHIFT].wait()
        norm[0:1, :] = group_mean
        norm[1:2, :] = scale
        norm[2:3, :] = gain[...].reshape(1, CH)
        norm[3:4, :] = shift[...].reshape(1, CH)
        for r in (1, 2, 3):
            activate(r)

        load[D_TW].wait()
        load[D_STEP].wait()
        features_half = tw.shape[0] // 2
        j = lax.broadcasted_iota(jnp.int32, (16, features_half), 1).astype(F32)
        angle = timestep[0].astype(F32) * jnp.exp(j * (-math.log(10000.0) / features_half))
        cos, sin = jnp.cos(angle), jnp.sin(angle)
        cos = (cos / (1.0 + jnp.exp(-cos))).astype(BF16)
        sin = (sin / (1.0 + jnp.exp(-sin))).astype(BF16)
        time_shift = jnp.dot(cos, tw[0:features_half, :], preferred_element_type=F32) + jnp.dot(
            sin, tw[features_half:, :], preferred_element_type=F32
        )

        load[D_CONV].wait()
        conv_acc[...] = jnp.broadcast_to(time_shift[0:1], (TOK, CH))
        convolve(ROW, 0, TOK, 1)
        got("z0", "z1")
        go("pr0", "pl0")
        convolve(ROW, ROW, 2 * ROW, 0)
        convolve(2 * ROW, 0, 2 * ROW, 2)

    def top_row():
        @pl.when(me > 0)
        def _():
            down.wait_recv()

        activate(0)
        convolve(0, 0, ROW, 0)

    def bottom_row():
        @pl.when(me < PATCHES - 1)
        def _():
            up.wait_recv()

        activate(4)
        convolve(4 * ROW, 2 * ROW, ROW, 2)

    def one_step(step, carry):
        @pl.when(step == 1)
        def _():
            combine_ring()

            @pl.when(zh == 0)
            def _():
                pl.semaphore_wait(late_sem, 1)

            stat_p.start()

            @pl.when(zh == 0)
            def _():
                go("z0")

            go("z1", "z2", "z3")

            got("r0", "l1")
            go("or", "ol")

            @pl.when(me < PATCHES - 1)
            def _():
                down.start()

            @pl.when(me > 0)
            def _():
                up.start()

        @pl.when(step == 2)
        def _():
            got("r1", "l0")

        @pl.when(step == 3)
        def _():
            inner_rows()
            got("or", "ol")

            @pl.when(me == 0)
            def _():
                down.wait_recv()
                relay.start()

            @pl.when(me == PATCHES - 1)
            def _():
                up.wait_recv()
                relay_up.start()

            go("oz")


        @pl.when(step == 4)
        def _():
            got("z2")
            go("pr2", "pl2")
            got("pr0", "pl0")
            go("po0", "po1")

        @pl.when(step == 5)
        def _():
            got("z3")
            go("pr3", "pl3")
            got("pr2")
            go("po2")

        @pl.when(step == 6)
        def _():
            got("pl2", "po0", "po1")

        @pl.when(step == 7)
        def _():
            @pl.when(me != RING)
            def _():
                top_row()

            @pl.when(me != RING - 1)
            def _():
                bottom_row()

            got("pr3", "pl3", "po2", "oz")

        attend(step)
        return carry

    lax.fori_loop(0, PATCHES, one_step, 0)


    for p in range(PAIRS):
        total = acc[p]
        first = total[0:64, 0:TOK] / total[PAIR_CH : PAIR_CH + 1, 0:TOK]
        second = total[64:128, TOK:PAIR_Q] / total[PAIR_CH : PAIR_CH + 1, TOK:PAIR_Q]
        attn_ref[:, PAIR_CH * p : PAIR_CH * (p + 1)] = jnp.concatenate([first, second], axis=0).T.astype(BF16)

    @pl.when(me == RING)
    def _():
        top_row()

    @pl.when(me == RING - 1)
    def _():
        bottom_row()

    res_ref[...] = conv_acc[...].astype(BF16)

    for copy in (stat_r, stat_l, stat_o, stat_p):
        copy.wait_send()

    @pl.when(me == 0)
    def _():
        relay.wait_send()

    @pl.when(me == PATCHES - 1)
    def _():
        relay_up.wait_send()

    @pl.when(me < PATCHES - 1)
    def _():
        down.wait_send()

    @pl.when(me > 0)
    def _():
        up.wait_send()

    for name, copy in bulks.items():
        copy.wait_send()


def hand_on(res, attn, res_out, attn_out):
    res_out[...] = res[...]
    attn_out[...] = attn[...]


def per_device(timestep, features, hidden, stale_hidden, gn_gain, gn_shift, conv_kernel, time_weight, wq, wk, wv):
    anywhere = pl.BlockSpec(memory_space=pl.ANY)
    vmem = pl.BlockSpec(memory_space=pltpu.VMEM)
    out = jax.ShapeDtypeStruct((TOK, CH), BF16)
    made = pl.pallas_call(
        kernel,
        out_shape=(out, out),
        in_specs=[anywhere] * 11,
        out_specs=(vmem, vmem),
        scratch_shapes=[
            pltpu.VMEM((PATCHES, TOK, CH), BF16),
            pltpu.VMEM((TOK + 2 * ROW, CH), BF16),
            pltpu.VMEM((6, 8, CH), F32),
            pltpu.VMEM((CH, CH), BF16),
            pltpu.VMEM((CH, CH), BF16),
            pltpu.VMEM((CH, CH), BF16),
            pltpu.VMEM((CH, CH), BF16),
            pltpu.VMEM((320, CH), BF16),
            pltpu.VMEM((3, 3 * CH, CH), BF16),
            pltpu.VMEM((TOK + 2 * ROW, 3 * CH), BF16),
            pltpu.VMEM((PAIRS, PAIR_CH, PAIR_Q), BF16),
            pltpu.VMEM((TOK, CH), BF16),
            pltpu.VMEM((PAIRS, VROWS, TOK), BF16),
            pltpu.VMEM((2, TOK, PAIR_Q), F32),
            pltpu.VMEM((2, TOK, PAIR_Q), BF16),
            pltpu.VMEM((PAIRS, 1, PAIR_Q), F32),
            pltpu.VMEM((PAIRS, VROWS, PAIR_Q), F32),
            pltpu.VMEM((TOK, CH), F32),
            pltpu.VMEM((8, CH), F32),
            pltpu.VMEM((CH,), F32),
            pltpu.VMEM((CH,), F32),
            pltpu.SMEM((1,), jnp.int32),
            pltpu.SemaphoreType.DMA((N_SENDS,)),
            pltpu.SemaphoreType.DMA((6,)),
            pltpu.SemaphoreType.DMA((PATCHES, 8)),
            pltpu.SemaphoreType.DMA((10,)),
            pltpu.SemaphoreType.REGULAR,
        ],
        compiler_params=pltpu.CompilerParams(
            collective_id=0, has_side_effects=True, vmem_limit_bytes=56 * 2**20
        ),
    )(
        timestep, features, hidden, stale_hidden, gn_gain, gn_shift,
        conv_kernel.reshape(3, 3 * CH, CH), time_weight, wq, wk, wv,
    )
    return pl.pallas_call(
        hand_on,
        out_shape=(out, out),
        in_specs=[vmem, vmem],
        out_specs=(vmem, vmem),
    )(*made)


def solution(mesh):
    tokens = P(("batch", "patch"), None)
    return jax.shard_map(
        per_device,
        mesh=mesh,
        in_specs=(P("batch"), tokens, tokens, tokens) + (P(),) * 7,
        out_specs=(tokens, tokens),
        check_vma=False,
    )
```
